32 devices in a mesh: sx: 8 (over y, x, core), sy: 4 (over z).
Axes of the slice: x: 2, y: 2, z: 4, core: 2. Of those that a mesh axis runs over, the one named last changes fastest.
Arguments:
- forward_prop: bfloat16 [2, 2, 12, 12, 64, 4096], P(None, None, None, None, 'sx', 'sy'), may hold values from -0.08984375 to 0.08984375
- backward_prop: bfloat16 [2, 2, 12, 12, 64, 4096], P(None, None, None, None, 'sx', 'sy'), may hold values from -0.08984375 to 0.08984375
- gamma_table: int32 [16, 4, 2], replicated, may hold values from 0 to 3, as said below
- source_site: int32 [3], replicated, may hold values from 0 to 63
- momenta: int32 [32, 3], replicated, may hold values from -8 to 7
Outputs:
- corr: float32 [16, 2, 2, 64, 4096], P(None, None, None, 'sx', 'sy')
- listed: float32 [2, 16, 2, 32], replicated
The draws below stay inside these ranges and needn't reach their ends.
Inputs may be any that keep to these rules, and one draw needn't show every extreme that they name: For every insertion g, gamma_table[g, 0..3, 0] is a permutation of 0..3; gamma_table[g, s, 1] is the power of i of that entry.
All inputs are finite; a program needn't handle non-finite values.
Results may differ from the reference program's by a relative error of at most 0.0003.
Values sent between devices are 32-bit elements; how exact they have to be, the bound alone decides.
No kernel may reach another device: no remote copies, remote signals or barrier semaphores. Data moves between devices by JAX's collectives and lax.ppermute only.
A program may use at most 384 MiB of HBM per device.

```python
import math
import jax
import jax.numpy as jnp
from jax import lax

L = 64
LZ = 64
G = 16
TW = 2
NMOM = 32


def draw_gamma_table(key, part):
    perm_key, phase_key = jax.random.split(jax.random.fold_in(key, 7))
    row_keys = jax.random.split(perm_key, G)
    columns = jax.vmap(lambda single: jax.random.permutation(single, 4))(row_keys)
    powers = jax.random.randint(phase_key, (G, 4), 0, 4)
    return jnp.stack([columns.astype(jnp.int32), powers.astype(jnp.int32)], -1)


def touch_ends(entries, key, smallest, largest):
    longest = entries.shape.index(max(entries.shape))
    spots = []
    for shift in (0, 1):
        where = [jax.random.randint(jax.random.fold_in(key, axis), (), 0, length) for axis, length in enumerate(entries.shape)]
        where[longest] = (where[longest] + shift) % entries.shape[longest]
        spots.append(tuple(where))
    return entries.at[spots[0]].set(smallest).at[spots[1]].set(largest)


def block_scale(rng, dims, shards, least, high):
    def one(position, parts):
        heights = jax.random.uniform(jax.random.fold_in(jax.random.fold_in(rng, 6), position), (parts,), jnp.float32, least / len(shards), high / len(shards))
        return jnp.repeat(jnp.exp(heights), dims[position] // parts).reshape((-1,) + (1,) * (len(dims) - position - 1))

    loudness = one(*shards[0])
    for cut in shards[1:]:
        loudness = loudness * one(*cut)
    return loudness


def scatter_about(rng, shape, width, limit, pieces=(), kind=jnp.bfloat16):
    drawn = width * jax.random.normal(rng, shape, jnp.float32)
    if pieces:
        drawn = drawn * block_scale(rng, shape, pieces, -0.22, 0.18)
    return jnp.clip(drawn, -limit, limit).astype(kind)


def setup_inputs(seed: int = 0) -> dict:
    arg_keys = jax.random.split(jax.random.key(seed), 6)
    forward_prop = scatter_about(arg_keys[0], (TW, 2, 12, 12, L, L * LZ), 0.015, 0.08984375, ((4, 8), (5, 4)))
    backward_prop = scatter_about(arg_keys[1], (TW, 2, 12, 12, L, L * LZ), 0.015, 0.08984375, ((4, 8), (5, 4)))
    gamma_table = draw_gamma_table(jax.random.fold_in(arg_keys[5], 71), 0)
    source_site = jax.random.randint(arg_keys[3], (3,), 0, LZ).astype(jnp.int32)
    momenta = touch_ends(jax.random.randint(arg_keys[4], (NMOM, 3), -8, 8), jax.random.fold_in(arg_keys[4], 1), -8, 7).astype(jnp.int32)
    return dict(forward_prop=forward_prop, backward_prop=backward_prop, gamma_table=gamma_table, source_site=source_site, momenta=momenta)


HIGHEST = lax.Precision.HIGHEST


def gamma_matrices(gamma_table):
    inserts = gamma_table.shape[0]
    columns = gamma_table[:, :, 0]
    powers = gamma_table[:, :, 1]
    spin_ids = jnp.arange(4, dtype=jnp.int32)
    matches = (columns[:, :, None] == spin_ids[None, None, :]).astype(jnp.float32)
    unit_re = (powers == 0).astype(jnp.float32) - (powers == 2).astype(jnp.float32)
    unit_im = (powers == 1).astype(jnp.float32) - (powers == 3).astype(jnp.float32)
    return (matches * unit_re[:, :, None]).reshape(inserts, 16), (matches * unit_im[:, :, None]).reshape(inserts, 16)


def reference(forward_prop, backward_prop, gamma_table, source_site, momenta):
    mat_re, mat_im = gamma_matrices(gamma_table)
    volume = L * L * LZ
    wave_xy = jnp.arange(L, dtype=jnp.int32)
    wave_z = jnp.arange(LZ, dtype=jnp.int32)
    index_xy = jnp.mod(wave_xy[:, None] * source_site[0] + wave_xy[None, :] * source_site[1], L)
    index_z = jnp.mod(wave_z * source_site[2], LZ)
    angles = (2.0 * math.pi / L) * index_xy.astype(jnp.float32)[:, :, None] + (2.0 * math.pi / LZ) * index_z.astype(jnp.float32)[None, None, :]
    rotate = jnp.cos(angles) + 1j * jnp.sin(angles)
    pattern = "scjn,ucjn->sun"

    def one_slice(which):
        forward = lax.dynamic_index_in_dim(forward_prop, which, 0, keepdims=False).astype(jnp.float32)
        backward = lax.dynamic_index_in_dim(backward_prop, which, 0, keepdims=False).astype(jnp.float32)
        forward = forward.reshape(2, 4, 3, 12, volume)
        backward = backward.reshape(2, 4, 3, 12, volume)
        pair_re = jnp.einsum(pattern, backward[0], forward[0], precision=HIGHEST) + jnp.einsum(pattern, backward[1], forward[1], precision=HIGHEST)
        pair_im = jnp.einsum(pattern, backward[0], forward[1], precision=HIGHEST) - jnp.einsum(pattern, backward[1], forward[0], precision=HIGHEST)
        pair_re = pair_re.reshape(16, volume)
        pair_im = pair_im.reshape(16, volume)
        field_re = jnp.dot(mat_re, pair_re, precision=HIGHEST) - jnp.dot(mat_im, pair_im, precision=HIGHEST)
        field_im = jnp.dot(mat_re, pair_im, precision=HIGHEST) + jnp.dot(mat_im, pair_re, precision=HIGHEST)
        field = (field_re + 1j * field_im).reshape(G, L, L, LZ)
        spectrum = jnp.fft.fftn(field, axes=(1, 2, 3)) * rotate[None]
        return spectrum.real.astype(jnp.float32), spectrum.imag.astype(jnp.float32)

    spec_re, spec_im = lax.map(one_slice, jnp.arange(TW, dtype=jnp.int32))
    corr = jnp.stack([spec_re, spec_im], 2).transpose(1, 0, 2, 4, 5, 3).reshape(G, TW, 2, L, LZ * L)
    mom_x = jnp.mod(momenta[:, 0], L)
    mom_y = jnp.mod(momenta[:, 1], L)
    mom_z = jnp.mod(momenta[:, 2], LZ)
    pick_re = spec_re[:, :, mom_x, mom_y, mom_z].transpose(1, 0, 2)
    pick_im = spec_im[:, :, mom_x, mom_y, mom_z].transpose(1, 0, 2)
    listed = jnp.stack([pick_re, pick_im], 0)
    return corr, listed
```

```python
import functools
import math

import jax
import jax.numpy as jnp
import ml_dtypes
import numpy as np
from jax import lax
from jax.experimental import pallas as pl
from jax.experimental.pallas import tpu as pltpu
from jax.sharding import PartitionSpec as P

L = 64
LZ = 64


HIGHEST = lax.Precision.HIGHEST


def gamma_matrices(gamma_table):
    inserts = gamma_table.shape[0]
    columns = gamma_table[:, :, 0]
    powers = gamma_table[:, :, 1]
    spin_ids = jnp.arange(4, dtype=jnp.int32)
    matches = (columns[:, :, None] == spin_ids[None, None, :]).astype(jnp.float32)
    unit_re = (powers == 0).astype(jnp.float32) - (powers == 2).astype(jnp.float32)
    unit_im = (powers == 1).astype(jnp.float32) - (powers == 3).astype(jnp.float32)
    return (
        (matches * unit_re[:, :, None]).reshape(inserts, 16),
        (matches * unit_im[:, :, None]).reshape(inserts, 16),
    )


def dft_table(length, anchor):
    wavenum = jnp.arange(length, dtype=jnp.int32)
    offsets = jnp.mod(wavenum - anchor, length)
    phase_index = jnp.mod(offsets[:, None] * wavenum[None, :], length)
    angles = 2.0 * math.pi / length * phase_index.astype(jnp.float32)
    return (jnp.cos(angles), -jnp.sin(angles))


def complex_step(real_part, imag_part, table_re, table_im, pattern):
    out_re = jnp.einsum(pattern, real_part, table_re, precision=HIGHEST) - jnp.einsum(
        pattern, imag_part, table_im, precision=HIGHEST
    )
    out_im = jnp.einsum(pattern, real_part, table_im, precision=HIGHEST) + jnp.einsum(
        pattern, imag_part, table_re, precision=HIGHEST
    )
    return (out_re, out_im)


def transform(fields, source_site):
    table_re, table_im = dft_table(fields.shape[4], source_site[2])
    along_z = jnp.stack(
        complex_step(fields[:, 0], fields[:, 1], table_re, table_im, "nabz,zk->nabk"), 1
    )
    depth_share = along_z.shape[4] // lax.axis_size("sy")
    first_depth = lax.axis_index("sy") * depth_share
    length_y = along_z.shape[3] * lax.axis_size("sy")
    full_re, full_im = dft_table(length_y, source_site[1])
    part = lax.dynamic_slice_in_dim(
        lax.all_gather(along_z, "sy", axis=3, tiled=True), first_depth, depth_share, 4
    )
    step_re, step_im = complex_step(part[:, 0], part[:, 1], full_re, full_im, "nayc,yk->nakc")
    along_y = jnp.stack([step_re, step_im], 1)
    arrived = lax.all_to_all(along_y, "sx", split_axis=3, concat_axis=2, tiled=True)
    table_re, table_im = dft_table(arrived.shape[2], source_site[0])
    along_x = complex_step(arrived[:, 0], arrived[:, 1], table_re, table_im, "nxbc,xk->nbck")
    return jnp.stack(along_x, 1)


def apply_gammas(mat_re, mat_im, real_part, imag_part):
    extent = real_part.shape
    flat_re = real_part.reshape(extent[0], -1)
    flat_im = imag_part.reshape(extent[0], -1)
    out_re = jnp.dot(mat_re, flat_re, precision=HIGHEST) - jnp.dot(
        mat_im, flat_im, precision=HIGHEST
    )
    out_im = jnp.dot(mat_re, flat_im, precision=HIGHEST) + jnp.dot(
        mat_im, flat_re, precision=HIGHEST
    )
    return (out_re.reshape(extent), out_im.reshape(extent))


def project_sites(fields, source_site, momenta, rows_x, rows_y, length, depth):
    coord_x = lax.axis_index("sx") * rows_x + jnp.arange(rows_x, dtype=jnp.int32) - source_site[0]
    coord_y = lax.axis_index("sy") * rows_y + jnp.arange(rows_y, dtype=jnp.int32) - source_site[1]
    coord_z = jnp.arange(depth, dtype=jnp.int32) - source_site[2]
    part_x = jnp.mod(momenta[:, 0:1] * coord_x[None, :], length)
    part_y = jnp.mod(momenta[:, 1:2] * coord_y[None, :], length)
    part_z = jnp.mod(momenta[:, 2:3] * coord_z[None, :], depth)
    plane = jnp.mod(part_x[:, :, None] + part_y[:, None, :], length).astype(jnp.float32)
    angles = (
        2.0 * math.pi / length * plane[:, :, :, None]
        + 2.0 * math.pi / depth * part_z.astype(jnp.float32)[:, None, None, :]
    )
    angles = angles.reshape(momenta.shape[0], -1)
    cosine = jnp.cos(angles)
    sine = jnp.sin(angles)
    field_re = fields[:, 0].reshape(fields.shape[0], -1)
    field_im = fields[:, 1].reshape(fields.shape[0], -1)
    local_re = jnp.dot(field_re, cosine.T, precision=HIGHEST) + jnp.dot(
        field_im, sine.T, precision=HIGHEST
    )
    local_im = jnp.dot(field_im, cosine.T, precision=HIGHEST) - jnp.dot(
        field_re, sine.T, precision=HIGHEST
    )
    return (local_re, local_im)


def general_body(forward_prop, backward_prop, gamma_table, source_site, momenta):
    slices = forward_prop.shape[0]
    rows_x = forward_prop.shape[4]
    rows_y = backward_prop.shape[5] // LZ
    inserts = gamma_table.shape[0]
    forward = forward_prop.reshape(slices, 2, 4, 3, 12, -1)
    backward = backward_prop.reshape(slices, 2, 4, 3, 12, -1)
    pattern = "tscjn,tucjn->sutn"
    pair_re = jnp.einsum(
        pattern, backward[:, 0], forward[:, 0], preferred_element_type=jnp.float32
    ) + jnp.einsum(pattern, backward[:, 1], forward[:, 1], preferred_element_type=jnp.float32)
    pair_im = jnp.einsum(
        pattern, backward[:, 0], forward[:, 1], preferred_element_type=jnp.float32
    ) - jnp.einsum(pattern, backward[:, 1], forward[:, 0], preferred_element_type=jnp.float32)
    pair_re = pair_re.reshape(16, slices, -1)
    pair_im = pair_im.reshape(16, slices, -1)
    mat_re, mat_im = gamma_matrices(gamma_table)
    field_re, field_im = apply_gammas(mat_re, mat_im, pair_re, pair_im)
    fields = jnp.stack([field_re, field_im], 2).reshape(inserts * slices, 2, rows_x, rows_y, LZ)
    spectrum = transform(fields, source_site)
    local_re, local_im = project_sites(fields, source_site, momenta, rows_x, rows_y, L, LZ)
    listed_re, listed_im = lax.psum((local_re, local_im), ("sx", "sy"))
    listed_re = listed_re.reshape(inserts, slices, -1)
    listed_im = listed_im.reshape(inserts, slices, -1)
    corr_re = spectrum[:, 0].reshape(inserts, slices, spectrum.shape[2], -1)
    corr_im = spectrum[:, 1].reshape(inserts, slices, spectrum.shape[2], -1)
    return (jnp.stack([corr_re, corr_im], 2), jnp.stack([listed_re, listed_im], 0))


F32 = jnp.float32
BF16 = jnp.bfloat16
MIB = 2**20


def split_table(table):
    high = table.astype(ml_dtypes.bfloat16)
    low = (table - high.astype(np.float64)).astype(ml_dtypes.bfloat16)
    return (high, low)


def split(values):
    high = values.astype(BF16)
    return (high, (values - high.astype(F32)).astype(BF16))


def turn(out_wave, in_site):
    angle = 2.0 * math.pi / L * np.mod(np.multiply.outer(out_wave, in_site), L)
    cosine, sine = (np.cos(angle), np.sin(angle))
    table = np.empty((len(out_wave), 2, 2, len(in_site)))
    table[:, 0, 0] = cosine
    table[:, 0, 1] = sine
    table[:, 1, 0] = -sine
    table[:, 1, 1] = cosine
    return table


def table_z():
    wave = turn(np.arange(64), np.arange(64)).reshape(4, 2, 4, 2, 2, 2, 64)
    full = np.zeros((4, 2, 4, 2, 2, 2, 2, 2, 64))
    for y in range(2):
        full[:, :, :, :, :, y, :, y, :] = wave
    return split_table(full.reshape(4, 64, 256))


def table_y():
    wave = turn(np.arange(64), np.arange(64)).reshape(8, 8, 2, 2, 4, 8, 2)
    full = np.zeros((4, 8, 2, 2, 8, 4, 8, 2, 2, 2))
    for position in range(4):
        for step in range(4):
            source = position ^ step
            for p in range(2):
                full[position, :, p, :, :, step, :, p] = wave[:, :, :, :, source].transpose(
                    0, 2, 1, 4, 3, 5
                )
    return split_table(full.reshape(4, 256, 256))


def table_x():
    wave = turn(np.arange(64), np.arange(64))
    cosine, sine = (wave[:, 0, 0].T, wave[:, 0, 1].T)
    high, low = split_table(np.concatenate([cosine, cosine, sine, sine], 1))
    return np.concatenate([high, high, low], 0)


def nt_dot(a, b):
    return lax.dot_general(a, b, (((1,), (1,)), ((), ())), preferred_element_type=F32)


def nn_dot(a, b):
    return lax.dot_general(a, b, (((1,), (0,)), ((), ())), preferred_element_type=F32)


def tn_dot(a, b):
    return lax.dot_general(a, b, (((0,), (0,)), ((), ())), preferred_element_type=F32)


def contract_block(f_ref, b_ref, lanes):
    def add(total, term):
        return term if total is None else total + term

    def load(ref, ri, row, pair):
        both = ref[0, ri, row, 2 * pair : 2 * pair + 2, :, lanes].astype(F32)
        return (both[0], both[1])

    real, imag = ([None] * 16, [None] * 16)
    for colour in range(3):
        for pair in range(6):
            back = [[load(b_ref, ri, 3 * s + colour, pair) for ri in (0, 1)] for s in range(4)]
            forw = [[load(f_ref, ri, 3 * u + colour, pair) for ri in (0, 1)] for u in range(4)]
            for h in (0, 1):
                for s in range(4):
                    b_re, b_im = (back[s][0][h], back[s][1][h])
                    for u in range(4):
                        f_re, f_im = (forw[u][0][h], forw[u][1][h])
                        k = 4 * s + u
                        real[k] = add(real[k], b_re * f_re + b_im * f_im)
                        imag[k] = add(imag[k], b_re * f_im - b_im * f_re)
    return (real, imag)


def pair_kernel(first, halves, f_ref, b_ref, high_ref, low_ref, *rest):
    pos = lax.axis_index("sy")
    if first == "listed":
        (old_ref, tm_high_ref, tm_low_ref, rot_ref, last_ref) = rest[:5]
        rest = rest[5:]
    elif first == "again":
        rest = rest[1:]
    sends = [rest[4 * h : 4 * h + 4] for h in range(halves)]
    rest = rest[4 * halves :]
    field_ref = rest[0]
    step = pl.program_id(0)
    w_high = jnp.concatenate([high_ref[pos ^ s] for s in range(4)], 0)
    w_low = jnp.concatenate([low_ref[pos ^ s] for s in range(4)], 0)
    for part in range(2):
        lanes = pl.ds(128 * part, 128)
        real, imag = contract_block(f_ref, b_ref, lanes)
        for k in range(16):
            field_ref[k, 0, :, lanes] = real[k]
            field_ref[k, 1, :, lanes] = imag[k]

    def planes(ref, part):
        lanes = pl.ds(128 * part, 128)
        re_high, re_low = split(ref[:, 0, :, lanes].reshape(128, 128))
        im_high, im_low = split(ref[:, 1, :, lanes].reshape(128, 128))
        return (
            jnp.concatenate([re_high, im_high], 1),
            jnp.concatenate([re_low, im_low], 1),
        )

    if first == "listed":
        total_ref = rest[1]

        @pl.when(step == 0)
        def _():
            total_ref[...] = jnp.zeros_like(total_ref)

    for part in range(2):
        high, low = planes(field_ref, part)
        out = nt_dot(w_high, high) + nt_dot(w_low, high) + nt_dot(w_high, low)
        out = out.reshape(4, halves, 8 // halves, 8, 128)
        row = 2 * step + part
        for s in range(4):
            for h in range(halves):
                if first == "listed" and h == 0:
                    sends[h][s][pl.ds(4 * row, 4)] = out[s, h]
                else:
                    sends[h][s][row] = out[s, h]
        if first == "listed":
            for t, source in enumerate((old_ref, field_ref)):
                if t == 0:
                    high, low = planes(old_ref, part)
                else:
                    high, low = planes(field_ref, part)
                proj = (
                    nn_dot(high, tm_high_ref[...])
                    + nn_dot(high, tm_low_ref[...])
                    + nn_dot(low, tm_high_ref[...])
                )
                value, turned = (proj[:, :128], proj[:, 128:])
                cosine = rot_ref[row, 0:1]
                sine = rot_ref[row, 1:2]
                total_ref[t, 0] += cosine * value + sine * turned
                total_ref[t, 1] += cosine * turned - sine * value

    if first == "listed":

        @pl.when(step == pl.num_programs(0) - 1)
        def _():
            upper = lax.broadcasted_iota(jnp.int32, (8, 128), 1) >= 64
            for t in range(2):
                value = total_ref[t, 0].reshape(16, 8, 128)
                turned = total_ref[t, 1].reshape(16, 8, 128)
                phased = value * last_ref[0][None] + turned * last_ref[1][None]
                summed = jnp.sum(phased, 1)
                tile = jnp.where(upper, summed[8:], summed[:8])
                for s in range(4):
                    sends[0][s][32 + t] = tile


def pair_call(first, which, start, rows, halves, forward, backward, tables, extra):
    steps = rows // 2
    high, low = tables

    def block(step):
        return (which, 0, 0, 0, 0, start // 2 + step)

    def field_block(step):
        return (0, 0, 0, start // 2 + step)

    def whole(shape):
        return pl.BlockSpec(shape, lambda step: (0,) * len(shape))

    in_specs = [pl.BlockSpec((1, 2, 12, 12, 8, 256), block)] * 2 + [whole((4, 64, 256))] * 2
    operands = [forward, backward, high, low]
    shapes = []
    for h in range(halves):
        shape = (rows, 8 // halves, 8, 128)
        if first == "listed" and h == 0:
            shape = (4 * rows + 2, 8, 128)
        shapes += [shape] * 4
    out_shape = [jax.ShapeDtypeStruct(shape, F32) for shape in shapes]
    out_specs = [whole(shape) for shape in shapes]
    fields = jax.ShapeDtypeStruct((16, 2, 8, 1024), F32)
    field_spec = pl.BlockSpec((16, 2, 8, 256), field_block)
    aliases = {}
    scratch = []
    if first == "listed":
        in_specs += [field_spec] + [whole(x.shape) for x in extra[1:]]
        operands += extra
        scratch = [pltpu.VMEM((16, 2, 8, 256), F32), pltpu.VMEM((2, 2, 128, 128), F32)]
    else:
        out_shape.append(fields)
        out_specs.append(field_spec)
        if first == "again":
            in_specs.append(pl.BlockSpec(memory_space=pl.ANY))
            operands += extra
            aliases = {4: len(out_shape) - 1}
    out = pl.pallas_call(
        functools.partial(pair_kernel, first, halves),
        grid=(steps,),
        in_specs=in_specs,
        out_specs=out_specs,
        out_shape=out_shape,
        scratch_shapes=scratch,
        input_output_aliases=aliases,
        compiler_params=pltpu.CompilerParams(vmem_limit_bytes=40 * MIB),
        cost_estimate=pl.CostEstimate(
            flops=rows * 1024 * 16 * 36 * 8, bytes_accessed=rows * 1024 * 1300, transcendentals=0
        ),
        name="contract_and_z",
    )(*operands)
    messages = [out[4 * h : 4 * h + 4] for h in range(halves)]
    return (messages, out[4 * halves :])


def y_kernel(parts, listed, *refs):
    messages = [refs[4 * part : 4 * part + 4] for part in range(parts)]
    high_ref, low_ref, send_ref, work_ref = refs[4 * parts :]
    rows = 8 // parts
    for q in range(4):
        data = []
        for s in range(4):
            for part in range(parts):
                ref = messages[part][s]
                if listed:
                    data += [ref[4 * yb + q] for yb in range(rows)]
                else:
                    data += [ref[yb, q] for yb in range(rows)]
        data = jnp.concatenate(data, 0)
        high, low = split(data)
        out = nn_dot(high_ref[...], high) + nn_dot(low_ref[...], high) + nn_dot(high_ref[...], low)
        work_ref[q] = out.reshape(8, 2, 2, 8, 128)
    for i in range(8):
        tiles = [work_ref[q, i, p, ri] for ri in range(2) for q in range(4) for p in range(2)]
        send_ref[i, 0:16] = jnp.concatenate(tiles, 0).T.reshape(16, 8, 128)
    if listed:
        ours = messages[0]
        for t in range(2):
            tile = (ours[0][32 + t] + ours[1][32 + t]) + (ours[2][32 + t] + ours[3][32 + t])
            for i in range(8):
                send_ref[i, 16 + t] = tile


def y_call(half, listed, messages, tables):
    high, low = tables

    def whole(shape):
        return pl.BlockSpec(shape, lambda step: (0,) * len(shape))

    in_specs = []
    operands = []
    for part in messages:
        for message in part:
            if half is None:
                in_specs.append(whole(message.shape))
            else:
                shape = (message.shape[0], 4, 8, 128)
                in_specs.append(pl.BlockSpec(shape, lambda step: (0, half, 0, 0)))
            operands.append(message)
    tiles = 18 if listed else 16
    return pl.pallas_call(
        functools.partial(y_kernel, len(messages), listed),
        grid=(1,),
        in_specs=in_specs + [whole((256, 256))] * 2,
        out_specs=whole((8, tiles, 8, 128)),
        out_shape=jax.ShapeDtypeStruct((8, tiles, 8, 128), F32),
        scratch_shapes=[pltpu.VMEM((4, 8, 2, 2, 8, 128), F32)],
        compiler_params=pltpu.CompilerParams(vmem_limit_bytes=32 * MIB),
        cost_estimate=pl.CostEstimate(
            flops=12 * 256 * 256 * 256, bytes_accessed=2**20, transcendentals=0
        ),
        name="along_y",
    )(*operands, high, low)


def x_kernel(listed, aliased, table_ref, data_ref, turn_ref, *refs):
    if aliased:
        refs = refs[1:]
    if listed:
        w_ref, out_ref, listed_ref, work_ref = refs
    else:
        w_ref, out_ref, work_ref = refs
    weights = w_ref[...]
    lower = lax.broadcasted_iota(jnp.int32, (8, 128), 1) < 64
    for f in range(16):
        high, low = split(data_ref[:, f].reshape(64, 128))
        out = tn_dot(jnp.concatenate([high, low, high], 0), weights)
        cosine = out[:, :128].reshape(2, 4, 2, 8, 128)
        sine = out[:, 128:].reshape(2, 4, 2, 8, 128)
        real = cosine[0] + sine[1]
        imag = cosine[1] - sine[0]
        for q in range(4):
            lanes = pl.ds(128 * q, 128)
            work_ref[f, 0, :, lanes] = jnp.where(lower, real[q, 0], real[q, 1])
            work_ref[f, 1, :, lanes] = jnp.where(lower, imag[q, 0], imag[q, 1])
    for g in range(16):
        real = jnp.zeros((8, 512), F32)
        imag = jnp.zeros((8, 512), F32)
        for s in range(4):
            field = 4 * s + table_ref[8 * g + 2 * s]
            power = table_ref[8 * g + 2 * s + 1]
            odd = power % 2
            sign_re = jnp.where((power == 0) | (power == 3), 1.0, -1.0).astype(F32)
            sign_im = jnp.where(power < 2, 1.0, -1.0).astype(F32)
            real += sign_re * work_ref[field, odd]
            imag += sign_im * work_ref[field, 1 - odd]
        cosine, sine = (turn_ref[0], turn_ref[1])
        out_ref[g, 0, 0] = real * cosine - imag * sine
        out_ref[g, 0, 1] = real * sine + imag * cosine
    if listed:
        for t in range(2):
            total = data_ref[0, 16 + t]
            for source in range(1, 8):
                total = total + data_ref[source, 16 + t]
            listed_ref[t] = total


def x_call(which, half, listed, data, gammas, turns, weights, corr):
    def whole(shape):
        return pl.BlockSpec(shape, lambda step: (0,) * len(shape))

    in_specs = [
        pl.BlockSpec(memory_space=pltpu.SMEM),
        whole(data.shape),
        pl.BlockSpec((2, 8, 512), lambda step: (0, 0, half)),
    ]
    operands = [gammas, data, turns]
    aliases = {}
    if corr is not None:
        aliases = {3: 0}
        in_specs.append(pl.BlockSpec(memory_space=pl.ANY))
        operands.append(corr)
    in_specs.append(whole(weights.shape))
    operands.append(weights)
    out_shape = [jax.ShapeDtypeStruct((16, 2, 2, 8, 1024), F32)]
    out_specs = [pl.BlockSpec((16, 1, 2, 8, 512), lambda step: (0, which, 0, 0, half))]
    if listed:
        out_shape.append(jax.ShapeDtypeStruct((2, 8, 128), F32))
        out_specs.append(whole((2, 8, 128)))
    return pl.pallas_call(
        functools.partial(x_kernel, listed, corr is not None),
        grid=(1,),
        in_specs=in_specs,
        out_specs=out_specs,
        out_shape=out_shape,
        scratch_shapes=[pltpu.VMEM((16, 2, 8, 512), F32)],
        input_output_aliases=aliases,
        compiler_params=pltpu.CompilerParams(vmem_limit_bytes=32 * MIB),
        cost_estimate=pl.CostEstimate(
            flops=6 * 16 * 128 * 64 * 256, bytes_accessed=2**20, transcendentals=0
        ),
        name="along_x",
    )(*operands)


def wave_angle(index):
    return 2.0 * math.pi / L * jnp.mod(index, L).astype(F32)


def momentum_tables(momenta, source_site):
    lane = jnp.arange(128, dtype=jnp.int32)
    mom = momenta[lane % 32]
    column = jnp.arange(256, dtype=jnp.int32)
    mom2 = momenta[column % 32]
    part_out = (column // 32) % 2
    turned = column // 128
    row = jnp.arange(256, dtype=jnp.int32)
    part_in = row // 128
    y = (row // 64) % 2
    z = row % 64
    index = y[:, None] * mom2[None, :, 1] + z[:, None] * mom2[None, :, 2]
    steps = index + 16 * (part_out + turned)[None, :] - 16 * part_in[:, None]
    table = jnp.cos(wave_angle(steps))
    high = lax.reduce_precision(table, 8, 7)
    tm_high, tm_low = (high.astype(BF16), (table - high).astype(BF16))
    pairs = jnp.arange(8, dtype=jnp.int32)
    angle = wave_angle(2 * pairs[:, None] * mom[None, :, 1])
    rot = jnp.stack([jnp.cos(angle), jnp.sin(angle)], 1)
    x = lax.axis_index("sx") * 8 + jnp.arange(8, dtype=jnp.int32) - source_site[0]
    rest = (lax.axis_index("sy") * 16 - source_site[1]) * mom[:, 1] - source_site[2] * mom[:, 2]
    angle = wave_angle(x[:, None] * mom[None, :, 0] + rest[None, :])
    last = jnp.stack([jnp.cos(angle), jnp.sin(angle)], 0)
    return [tm_high, tm_low, rot, last]


def source_turns(source_site):
    ky = lax.axis_index("sx") * 8 + jnp.arange(8, dtype=jnp.int32)
    kz = lax.axis_index("sy") * 16 + jnp.arange(16, dtype=jnp.int32)
    kx = jnp.arange(64, dtype=jnp.int32)
    index = (
        (ky * source_site[1])[:, None, None]
        + (kz * source_site[2])[None, :, None]
        + (kx * source_site[0])[None, None, :]
    )
    angle = wave_angle(index).reshape(8, 1024)
    return jnp.stack([jnp.cos(angle), jnp.sin(angle)], 0)


def swap_sy(message):
    out = [message[0]]
    for step in range(1, 4):
        out.append(lax.ppermute(message[step], "sy", [(k, k ^ step) for k in range(4)]))
    return out


def block_body(forward_prop, backward_prop, gamma_table, source_site, momenta):
    z_tables = [jnp.asarray(table) for table in table_z()]
    y_tables = [
        lax.dynamic_index_in_dim(jnp.asarray(table), lax.axis_index("sy"), 0, keepdims=False)
        for table in table_y()
    ]
    weights = jnp.asarray(table_x())
    gammas = gamma_table.reshape(-1)
    inputs = (forward_prop, backward_prop, z_tables)
    (first,), (fields,) = pair_call("first", 0, 0, 4, 1, *inputs, [])
    first = swap_sy(first)
    (second,), (fields,) = pair_call("again", 0, 4, 4, 1, *inputs, [fields])
    second = swap_sy(second)
    extra = [fields] + momentum_tables(momenta, source_site)
    messages, _ = pair_call("listed", 1, 0, 8, 2, *inputs, extra)
    third = swap_sy(messages[0])
    fourth = swap_sy(messages[1])
    turns = source_turns(source_site)
    corr = None
    chunks = [
        (0, 0, False, 0, [first, second]),
        (0, 1, False, 1, [first, second]),
        (1, 0, True, None, [third]),
        (1, 1, False, None, [fourth]),
    ]
    for which, half, listed, pick, parts in chunks:
        sent = y_call(pick, listed, parts, y_tables)
        data = lax.all_to_all(sent, "sx", 0, 0, tiled=True)
        out = x_call(which, half, listed, data, gammas, turns, weights, corr)
        corr = out[0]
        if listed:
            sums = out[1]
    sums = sums.reshape(2, 8, 2, 2, 32).transpose(0, 2, 1, 3, 4).reshape(2, 16, 2, 32)
    mat_re, mat_im = gamma_matrices(gamma_table)
    listed_re = jnp.einsum("gf,tfm->gtm", mat_re, sums[:, :, 0], precision=HIGHEST) - jnp.einsum(
        "gf,tfm->gtm", mat_im, sums[:, :, 1], precision=HIGHEST
    )
    listed_im = jnp.einsum("gf,tfm->gtm", mat_re, sums[:, :, 1], precision=HIGHEST) + jnp.einsum(
        "gf,tfm->gtm", mat_im, sums[:, :, 0], precision=HIGHEST
    )
    return (corr, jnp.stack([listed_re, listed_im], 0))


def body(forward_prop, backward_prop, gamma_table, source_site, momenta):
    sizes = (forward_prop.shape, lax.axis_size("sx"), lax.axis_size("sy"))
    fits = sizes == ((2, 2, 12, 12, 8, 16 * LZ), 8, 4) and L == 64 and LZ == 64
    fits = fits and gamma_table.shape[0] == 16 and momenta.shape[0] == 32
    run = block_body if fits else general_body
    return run(forward_prop, backward_prop, gamma_table, source_site, momenta)


def solution(mesh):
    placed = (
        P(None, None, None, None, "sx", "sy"),
        P(None, None, None, None, "sx", "sy"),
        P(),
        P(),
        P(),
    )
    return jax.shard_map(
        body,
        mesh=mesh,
        in_specs=placed,
        out_specs=(P(None, None, None, "sx", "sy"), P()),
        check_vma=False,
    )
```

```python
import functools
import math

import jax
import jax.numpy as jnp
import numpy as np
from jax import lax
from jax.experimental import pallas as pl
from jax.experimental.pallas import tpu as pltpu
from jax.sharding import PartitionSpec as P

L = 64
LZ = 64


HIGHEST = lax.Precision.HIGHEST


def gamma_matrices(gamma_table):
    inserts = gamma_table.shape[0]
    columns = gamma_table[:, :, 0]
    powers = gamma_table[:, :, 1]
    spin_ids = jnp.arange(4, dtype=jnp.int32)
    matches = (columns[:, :, None] == spin_ids[None, None, :]).astype(jnp.float32)
    unit_re = (powers == 0).astype(jnp.float32) - (powers == 2).astype(jnp.float32)
    unit_im = (powers == 1).astype(jnp.float32) - (powers == 3).astype(jnp.float32)
    return (
        (matches * unit_re[:, :, None]).reshape(inserts, 16),
        (matches * unit_im[:, :, None]).reshape(inserts, 16),
    )


def dft_table(length, anchor):
    wavenum = jnp.arange(length, dtype=jnp.int32)
    offsets = jnp.mod(wavenum - anchor, length)
    phase_index = jnp.mod(offsets[:, None] * wavenum[None, :], length)
    angles = 2.0 * math.pi / length * phase_index.astype(jnp.float32)
    return (jnp.cos(angles), -jnp.sin(angles))


def complex_step(real_part, imag_part, table_re, table_im, pattern):
    out_re = jnp.einsum(pattern, real_part, table_re, precision=HIGHEST) - jnp.einsum(
        pattern, imag_part, table_im, precision=HIGHEST
    )
    out_im = jnp.einsum(pattern, real_part, table_im, precision=HIGHEST) + jnp.einsum(
        pattern, imag_part, table_re, precision=HIGHEST
    )
    return (out_re, out_im)


def transform(fields, source_site):
    table_re, table_im = dft_table(fields.shape[4], source_site[2])
    along_z = jnp.stack(
        complex_step(fields[:, 0], fields[:, 1], table_re, table_im, "nabz,zk->nabk"), 1
    )
    depth_share = along_z.shape[4] // lax.axis_size("sy")
    first_depth = lax.axis_index("sy") * depth_share
    length_y = along_z.shape[3] * lax.axis_size("sy")
    full_re, full_im = dft_table(length_y, source_site[1])
    part = lax.dynamic_slice_in_dim(
        lax.all_gather(along_z, "sy", axis=3, tiled=True), first_depth, depth_share, 4
    )
    step_re, step_im = complex_step(part[:, 0], part[:, 1], full_re, full_im, "nayc,yk->nakc")
    along_y = jnp.stack([step_re, step_im], 1)
    arrived = lax.all_to_all(along_y, "sx", split_axis=3, concat_axis=2, tiled=True)
    table_re, table_im = dft_table(arrived.shape[2], source_site[0])
    along_x = complex_step(arrived[:, 0], arrived[:, 1], table_re, table_im, "nxbc,xk->nbck")
    return jnp.stack(along_x, 1)


def apply_gammas(mat_re, mat_im, real_part, imag_part):
    extent = real_part.shape
    flat_re = real_part.reshape(extent[0], -1)
    flat_im = imag_part.reshape(extent[0], -1)
    out_re = jnp.dot(mat_re, flat_re, precision=HIGHEST) - jnp.dot(
        mat_im, flat_im, precision=HIGHEST
    )
    out_im = jnp.dot(mat_re, flat_im, precision=HIGHEST) + jnp.dot(
        mat_im, flat_re, precision=HIGHEST
    )
    return (out_re.reshape(extent), out_im.reshape(extent))


def project_sites(fields, source_site, momenta, rows_x, rows_y, length, depth):
    coord_x = lax.axis_index("sx") * rows_x + jnp.arange(rows_x, dtype=jnp.int32) - source_site[0]
    coord_y = lax.axis_index("sy") * rows_y + jnp.arange(rows_y, dtype=jnp.int32) - source_site[1]
    coord_z = jnp.arange(depth, dtype=jnp.int32) - source_site[2]
    part_x = jnp.mod(momenta[:, 0:1] * coord_x[None, :], length)
    part_y = jnp.mod(momenta[:, 1:2] * coord_y[None, :], length)
    part_z = jnp.mod(momenta[:, 2:3] * coord_z[None, :], depth)
    plane = jnp.mod(part_x[:, :, None] + part_y[:, None, :], length).astype(jnp.float32)
    angles = (
        2.0 * math.pi / length * plane[:, :, :, None]
        + 2.0 * math.pi / depth * part_z.astype(jnp.float32)[:, None, None, :]
    )
    angles = angles.reshape(momenta.shape[0], -1)
    cosine = jnp.cos(angles)
    sine = jnp.sin(angles)
    field_re = fields[:, 0].reshape(fields.shape[0], -1)
    field_im = fields[:, 1].reshape(fields.shape[0], -1)
    local_re = jnp.dot(field_re, cosine.T, precision=HIGHEST) + jnp.dot(
        field_im, sine.T, precision=HIGHEST
    )
    local_im = jnp.dot(field_im, cosine.T, precision=HIGHEST) - jnp.dot(
        field_re, sine.T, precision=HIGHEST
    )
    return (local_re, local_im)


def general_body(forward_prop, backward_prop, gamma_table, source_site, momenta):
    slices = forward_prop.shape[0]
    rows_x = forward_prop.shape[4]
    rows_y = backward_prop.shape[5] // LZ
    inserts = gamma_table.shape[0]
    forward = forward_prop.reshape(slices, 2, 4, 3, 12, -1)
    backward = backward_prop.reshape(slices, 2, 4, 3, 12, -1)
    pattern = "tscjn,tucjn->sutn"
    pair_re = jnp.einsum(
        pattern, backward[:, 0], forward[:, 0], preferred_element_type=jnp.float32
    ) + jnp.einsum(pattern, backward[:, 1], forward[:, 1], preferred_element_type=jnp.float32)
    pair_im = jnp.einsum(
        pattern, backward[:, 0], forward[:, 1], preferred_element_type=jnp.float32
    ) - jnp.einsum(pattern, backward[:, 1], forward[:, 0], preferred_element_type=jnp.float32)
    pair_re = pair_re.reshape(16, slices, -1)
    pair_im = pair_im.reshape(16, slices, -1)
    mat_re, mat_im = gamma_matrices(gamma_table)
    field_re, field_im = apply_gammas(mat_re, mat_im, pair_re, pair_im)
    fields = jnp.stack([field_re, field_im], 2).reshape(inserts * slices, 2, rows_x, rows_y, LZ)
    spectrum = transform(fields, source_site)
    local_re, local_im = project_sites(fields, source_site, momenta, rows_x, rows_y, L, LZ)
    listed_re, listed_im = lax.psum((local_re, local_im), ("sx", "sy"))
    listed_re = listed_re.reshape(inserts, slices, -1)
    listed_im = listed_im.reshape(inserts, slices, -1)
    corr_re = spectrum[:, 0].reshape(inserts, slices, spectrum.shape[2], -1)
    corr_im = spectrum[:, 1].reshape(inserts, slices, spectrum.shape[2], -1)
    return (jnp.stack([corr_re, corr_im], 2), jnp.stack([listed_re, listed_im], 0))


F32 = jnp.float32
BF16 = jnp.bfloat16
MIB = 2**20


def split(values):
    high = values.astype(BF16)
    return (high, (values - high.astype(F32)).astype(BF16))


def turn(out_wave, in_site):
    angle = 2.0 * math.pi / L * np.mod(np.multiply.outer(out_wave, in_site), L)
    cosine, sine = (np.cos(angle), np.sin(angle))
    table = np.empty((len(out_wave), 2, 2, len(in_site)))
    table[:, 0, 0] = cosine
    table[:, 0, 1] = sine
    table[:, 1, 0] = -sine
    table[:, 1, 1] = cosine
    return table


def table_z():
    wave = turn(np.arange(64), np.arange(64)).reshape(4, 2, 4, 2, 2, 2, 64)
    full = np.zeros((4, 2, 4, 2, 2, 2, 2, 2, 64))
    for y in range(2):
        full[:, :, :, :, :, y, :, y, :] = wave
    return jnp.asarray(full.reshape(4, 64, 256).astype(np.float32))


def table_y():
    wave = turn(np.arange(64), np.arange(64)).reshape(8, 8, 2, 2, 4, 8, 2)
    full = np.zeros((4, 8, 2, 2, 8, 4, 8, 2, 2, 2))
    for position in range(4):
        for step in range(4):
            source = position ^ step
            for p in range(2):
                full[position, :, p, :, :, step, :, p] = wave[:, :, :, :, source].transpose(
                    0, 2, 1, 4, 3, 5
                )
    return jnp.asarray(full.reshape(4, 256, 256).astype(np.float32))


def table_x():
    wave = turn(np.arange(64), np.arange(64))
    cosine, sine = (wave[:, 0, 0].T, wave[:, 0, 1].T)
    table = np.concatenate([cosine, cosine, sine, sine], 1).astype(np.float32)
    return jnp.asarray(table.reshape(8, 8, 256))


def nt_dot(a, b):
    return lax.dot_general(a, b, (((1,), (1,)), ((), ())), preferred_element_type=F32)


def nn_dot(a, b):
    return lax.dot_general(a, b, (((1,), (0,)), ((), ())), preferred_element_type=F32)


def tn_dot(a, b):
    return lax.dot_general(a, b, (((0,), (0,)), ((), ())), preferred_element_type=F32)


def whole(shape):
    return pl.BlockSpec(shape, lambda step: (0,) * len(shape))


def cost(weight):
    return pl.CostEstimate(flops=weight * 10**13, bytes_accessed=0, transcendentals=0)


def contract_block(f_ref, b_ref):
    def add(total, term):
        return term if total is None else total + term

    def load(ref, ri, row, pair):
        both = ref[0, ri, row, 2 * pair : 2 * pair + 2].astype(F32)
        return (both[0], both[1])

    one, two, three = ([None] * 16, [None] * 16, [None] * 16)
    for colour in range(3):
        for pair in range(6):
            back = [[load(b_ref, ri, 3 * s + colour, pair) for ri in (0, 1)] for s in range(4)]
            forw = [[load(f_ref, ri, 3 * u + colour, pair) for ri in (0, 1)] for u in range(4)]
            for h in (0, 1):
                for s in range(4):
                    b_re, b_im = (back[s][0][h], back[s][1][h])
                    b_less, b_more = (b_re - b_im, b_re + b_im)
                    for u in range(4):
                        f_re, f_im = (forw[u][0][h], forw[u][1][h])
                        f_more = f_re + f_im
                        k = 4 * s + u
                        one[k] = add(one[k], b_re * f_more)
                        two[k] = add(two[k], b_less * f_im)
                        three[k] = add(three[k], b_more * f_re)
    return [(one[k] - two[k], one[k] - three[k]) for k in range(16)]


def phases(index):
    half = (((index + 32) & 63) - 32).astype(F32) * (math.pi / 64)
    square = half * half
    sine = jnp.full_like(square, -1 / math.factorial(11))
    for n in (9, 7, 5, 3, 1):
        sine = sine * square + (-1) ** (n // 2) / math.factorial(n)
    sine = sine * half
    cosine = jnp.full_like(square, 1 / math.factorial(12))
    for n in (10, 8, 6, 4, 2, 0):
        cosine = cosine * square + (-1) ** (n // 2) / math.factorial(n)
    return (1.0 - 2.0 * sine * sine, 2.0 * sine * cosine)


def iota(shape, dim):
    return lax.broadcasted_iota(jnp.int32, shape, dim)


def planes(ref):
    re_high, re_low = split(ref[:, 0].reshape(128, 128))
    im_high, im_low = split(ref[:, 1].reshape(128, 128))
    return (jnp.concatenate([re_high, im_high], 1), jnp.concatenate([re_low, im_low], 1))


def momentum_lanes(mom_ref):
    lane = iota((1, 128), 1) & 31
    rows = []
    for k in range(3):
        row = jnp.zeros((1, 128), jnp.int32)
        for m in range(32):
            row = jnp.where(lane == m, mom_ref[k, m], row)
        rows.append(row)
    return rows


def momentum_tables(mom_ref, tm_high_ref, tm_low_ref):
    _, mom_y, mom_z = momentum_lanes(mom_ref)
    out_part = ((iota((64, 128), 1) >> 5) & 1) == 1
    for y in range(2):
        cosine, sine = phases(mom_z * iota((64, 128), 0) + mom_y * y)
        less = jnp.where(out_part, cosine, sine)
        none = jnp.where(out_part, -sine, cosine)
        more = jnp.where(out_part, -cosine, -sine)
        for part_in, blocks in ((0, (none, more)), (1, (less, none))):
            for turned in range(2):
                high, low = split(blocks[turned])
                rows = pl.ds(128 * part_in + 64 * y, 64)
                lanes = pl.ds(128 * turned, 128)
                tm_high_ref[rows, lanes] = high
                tm_low_ref[rows, lanes] = low


def pair_kernel(start, apart, source_ref, mom_ref, f_ref, b_ref, wave_ref, *refs):
    sends = refs[:4] if apart else [refs[0].at[k] for k in range(4)]
    field_ref, w_high_ref, w_low_ref, tm_high_ref, tm_low_ref, total_ref = refs[4 if apart else 1 :]
    step = pl.program_id(0)

    @pl.when(step == 0)
    def _():
        blocks = [lax.axis_index("sy") ^ s if apart else s for s in range(4)]
        high, low = split(jnp.concatenate([wave_ref[block] for block in blocks], 0))
        w_high_ref[...] = high
        w_low_ref[...] = low
        momentum_tables(mom_ref, tm_high_ref, tm_low_ref)
        total_ref[...] = jnp.zeros_like(total_ref)

    for k, (real, imag) in enumerate(contract_block(f_ref, b_ref)):
        field_ref[k, 0] = real
        field_ref[k, 1] = imag
    high, low = planes(field_ref)
    out = nt_dot(w_high_ref[...], high) + nt_dot(w_low_ref[...], high) + nt_dot(w_high_ref[...], low)
    out = out.reshape(4, 8, 8, 128)
    for s in range(4):
        sends[s][pl.ds(8 * step, 8)] = out[s]
    proj = (
        nn_dot(high, tm_high_ref[...])
        + nn_dot(high, tm_low_ref[...])
        + nn_dot(low, tm_high_ref[...])
    )
    value, turned = (proj[:, :128], proj[:, 128:])
    mom_x, mom_y, mom_z = momentum_lanes(mom_ref)
    cosine, sine = phases(2 * mom_y * (start + step))
    total_ref[0] += cosine * value + sine * turned
    total_ref[1] += cosine * turned - sine * value

    @pl.when(step == pl.num_programs(0) - 1)
    def _():
        x = lax.axis_index("sx") * 8 - source_ref[0] + iota((8, 128), 0)
        rest = (lax.axis_index("sy") * 16 - source_ref[1]) * mom_y - source_ref[2] * mom_z
        cosine, sine = phases(x * mom_x + rest)
        value = total_ref[0].reshape(16, 8, 128)
        turned = total_ref[1].reshape(16, 8, 128)
        summed = jnp.sum(value * cosine[None] + turned * sine[None], 1)
        tile = jnp.where(iota((8, 128), 1) >= 64, summed[8:], summed[:8])
        for s in range(4):
            sends[s][sends[s].shape[0] - 1] = tile


def pair_call(which, start, rows, apart, forward, backward, wave, source_site, momenta):
    def block(step):
        return (which, 0, 0, 0, 0, start + step)

    shape = (8 * rows + 1, 8, 128)
    shapes = [shape] * 4 if apart else [(4, *shape)]
    out = pl.pallas_call(
        functools.partial(pair_kernel, start, apart),
        grid=(rows,),
        in_specs=[pl.BlockSpec(memory_space=pltpu.SMEM)] * 2
        + [pl.BlockSpec((1, 2, 12, 12, 8, 128), block)] * 2
        + [whole((4, 64, 256))],
        out_specs=[whole(shape) for shape in shapes],
        out_shape=[jax.ShapeDtypeStruct(shape, F32) for shape in shapes],
        scratch_shapes=[pltpu.VMEM((16, 2, 8, 128), F32)]
        + [pltpu.VMEM((256, 256), BF16)] * 4
        + [pltpu.VMEM((2, 128, 128), F32)],
        compiler_params=pltpu.CompilerParams(vmem_limit_bytes=62 * MIB),
        cost_estimate=cost(0),
        name="contract_and_z",
    )(source_site, momenta, forward, backward, wave)
    return out if apart else out[0]


def y_kernel(kinds, halves, apart_out, *refs):
    pos = lax.axis_index("sy")
    parts = []
    for apart in kinds:
        if apart:
            parts.append(refs[:4])
        else:
            parts.append([refs[0].at[pos ^ s] for s in range(4)])
        refs = refs[4 if apart else 1 :]
    wave_ref, *sends, work_ref = refs
    if not apart_out:
        sends = [sends[0].at[k] for k in range(8)]
    w_high, w_low = split(wave_ref[0])
    for q in range(4 * halves):
        data = []
        for s in range(4):
            for part in parts:
                data += [part[s][8 * y + q] for y in range(part[s].shape[0] // 8)]
        high, low = split(jnp.concatenate(data, 0))
        out = nn_dot(w_high, high) + nn_dot(w_low, high) + nn_dot(w_high, low)
        work_ref[q] = out.reshape(8, 2, 2, 8, 128)
    extra = sum(ref[ref.shape[0] - 1] for part in parts for ref in part)
    for h in range(halves):
        for step in range(8):
            block = lax.axis_index("sx") ^ step if apart_out else step
            tiles = [
                work_ref[4 * h + q, block, p, ri]
                for ri in range(2)
                for q in range(4)
                for p in range(2)
            ]
            turned = jnp.concatenate(tiles, 0).T.reshape(16, 8, 128)
            sends[step][pl.ds(16 * h, 16)] = turned
    for step in range(8):
        sends[step][sends[step].shape[0] - 1] = extra


def y_call(messages, wave, apart_out, micros):
    kinds = [isinstance(message, list) for message in messages]
    operands = [x for message in messages for x in (message if isinstance(message, list) else [message])]
    shapes = [(33, 8, 128)] * 8 if apart_out else [(8, 33, 8, 128)]
    return pl.pallas_call(
        functools.partial(y_kernel, kinds, 2, apart_out),
        grid=(1,),
        in_specs=[whole(x.shape) for x in operands]
        + [pl.BlockSpec((1, 256, 256), lambda step: (lax.axis_index("sy"), 0, 0))],
        out_specs=[whole(shape) for shape in shapes],
        out_shape=[jax.ShapeDtypeStruct(shape, F32) for shape in shapes],
        scratch_shapes=[pltpu.VMEM((8, 8, 2, 2, 8, 128), F32)],
        compiler_params=pltpu.CompilerParams(vmem_limit_bytes=32 * MIB),
        cost_estimate=cost(micros),
        name="along_y",
    )(*operands, wave)


def x_kernel(count, first_half, last, table_ref, source_ref, rows_ref, wave_ref, *refs):
    data_refs, work_ref = (refs[:count], refs[-1])
    listed_ref = refs[-2] if first_half == 0 else None
    out_ref = refs[-3] if first_half == 0 else refs[-2]
    if count == 1:
        data_refs = [data_refs[0].at[k] for k in range(8)]
    step = pl.program_id(0)
    half = first_half + step
    first_x, first_y = (lax.axis_index("sx") * 8, lax.axis_index("sy") * 16)
    blocks = [k if count == 1 else lax.axis_index("sx") ^ k for k in range(8)]
    w_high, w_low = split(jnp.concatenate([wave_ref[block] for block in blocks], 0))
    weights = jnp.concatenate([w_high, w_high, w_low], 0)
    lower = iota((8, 128), 1) < 64
    for f in range(16):
        high, low = split(jnp.concatenate([ref[16 * step + f] for ref in data_refs], 0))
        out = tn_dot(jnp.concatenate([high, low, high], 0), weights)
        cosine = out[:, :128].reshape(2, 4, 2, 8, 128)
        sine = out[:, 128:].reshape(2, 4, 2, 8, 128)
        real = cosine[0] + sine[1]
        imag = cosine[1] - sine[0]
        for q in range(4):
            lanes = pl.ds(128 * q, 128)
            work_ref[f, 0, :, lanes] = jnp.where(lower, real[q, 0], real[q, 1])
            work_ref[f, 1, :, lanes] = jnp.where(lower, imag[q, 0], imag[q, 1])
    column = iota((8, 512), 1)
    index = (first_x + iota((8, 512), 0)) * source_ref[1] + (column & 63) * source_ref[0]
    cosine, sine = phases(index + (first_y + 8 * half + (column >> 6)) * source_ref[2])
    for g in range(16):
        real = jnp.zeros((8, 512), F32)
        imag = jnp.zeros((8, 512), F32)
        for s in range(4):
            field = 4 * s + table_ref[8 * g + 2 * s]
            power = table_ref[8 * g + 2 * s + 1]
            odd = power & 1
            sign_re = jnp.where((power == 0) | (power == 3), 1.0, -1.0).astype(F32)
            sign_im = jnp.where(power < 2, 1.0, -1.0).astype(F32)
            real += sign_re * work_ref[field, odd]
            imag += sign_im * work_ref[field, 1 - odd]
        out_ref[g, 0, 0] = real * cosine - imag * sine
        out_ref[g, 0, 1] = real * sine + imag * cosine

    def listed_sums():
        total = sum(ref[ref.shape[0] - 1] for ref in data_refs)
        rows = jnp.concatenate([total[:, 32 * k : 32 * k + 32] for k in range(4)], 0)
        high, rest = split(rows)
        middle, low = split(rows - high.astype(F32))
        mix = mix_matrix(rows_ref[...]).astype(BF16)
        sums = nn_dot(mix, high) + nn_dot(mix, middle) + nn_dot(mix, low)
        if last:
            for ri in range(2):
                for g in range(16):
                    row = slice(16 * ri + g, 16 * ri + g + 1)
                    listed_ref[ri, g, 0:1] = refs[count][row, :]
                    listed_ref[ri, g, 1:2] = sums[row]
        else:
            listed_ref[...] = sums

    if first_half == 0:
        pl.when(step == 0)(listed_sums)


def x_call(which, half, halves, data, gammas, rows, source_site, wave, corr, listed):
    in_specs = [
        pl.BlockSpec(memory_space=pltpu.SMEM),
        pl.BlockSpec(memory_space=pltpu.SMEM),
        whole((16, 8)),
        whole((8, 8, 256)),
    ] + [whole(x.shape) for x in data]
    operands = [gammas, source_site, rows, wave, *data]
    aliases = {}
    if listed is not None:
        in_specs.append(whole((32, 32)))
        operands.append(listed)
    if corr is not None:
        aliases = {len(operands): 0}
        in_specs.append(pl.BlockSpec(memory_space=pl.ANY))
        operands.append(corr)
    shapes = [(16, 2, 2, 8, 1024)]
    out_specs = [pl.BlockSpec((16, 1, 2, 8, 512), lambda step: (0, which, 0, 0, half + step))]
    if half == 0:
        shapes.append((32, 32) if listed is None else (2, 16, 2, 32))
        out_specs.append(whole(shapes[1]))
    return pl.pallas_call(
        functools.partial(x_kernel, len(data), half, listed is not None),
        grid=(halves,),
        in_specs=in_specs,
        out_specs=out_specs,
        out_shape=[jax.ShapeDtypeStruct(shape, F32) for shape in shapes],
        scratch_shapes=[pltpu.VMEM((16, 2, 8, 512), F32)],
        input_output_aliases=aliases,
        compiler_params=pltpu.CompilerParams(vmem_limit_bytes=32 * MIB),
        cost_estimate=cost(0),
        name="along_x",
    )(*operands)


def mix_matrix(gammas):
    column = iota((16, 32), 1)
    field = (column >> 4) * 8 + (column & 7)
    on_imag = ((column >> 3) & 1) == 1
    real = jnp.zeros((16, 32), F32)
    imag = jnp.zeros((16, 32), F32)
    for s in range(4):
        match = field == 4 * s + gammas[:, 2 * s : 2 * s + 1]
        power = gammas[:, 2 * s + 1 : 2 * s + 2]
        unit_re = (power == 0).astype(F32) - (power == 2).astype(F32)
        unit_im = (power == 1).astype(F32) - (power == 3).astype(F32)
        real += jnp.where(match, jnp.where(on_imag, -unit_im, unit_re), 0.0)
        imag += jnp.where(match, jnp.where(on_imag, unit_re, unit_im), 0.0)
    return jnp.concatenate([real, imag], 0)


def swap_sy(message):
    out = [message[0]]
    for step in range(1, 4):
        out.append(lax.ppermute(message[step], "sy", [(k, k ^ step) for k in range(4)]))
    return out


def swap_sx_whole(message):
    return [lax.all_to_all(message[0], "sx", 0, 0, tiled=True)]


def swap_sx(message):
    out = [message[0]]
    for step in range(1, 8):
        out.append(lax.ppermute(message[step], "sx", [(k, k ^ step) for k in range(8)]))
    return out


def after(values, *others):
    return lax.optimization_barrier((values, others))[0]


def block_body(forward_prop, backward_prop, gamma_table, source_site, momenta):
    wave_z, wave_y, wave_x = (table_z(), table_y(), table_x())
    inputs = (forward_prop, backward_prop, wave_z, source_site, momenta.T)
    outer = (gamma_table.reshape(-1), gamma_table.reshape(16, 8), source_site, wave_x)
    first = pair_call(0, 0, 8, True, *inputs)
    inputs = after(inputs, first[0])
    first = swap_sy(first)
    third = pair_call(1, 0, 8, True, *inputs)
    first, third = after((first, third))
    third = swap_sy(third)
    sent = y_call([first], wave_y, False, 0)
    data = swap_sx_whole(sent)
    third = after(third, sent[0])
    sent = y_call([third], wave_y, True, 1)
    data = after(data, sent[0])
    corr, even = x_call(0, 0, 2, data, *outer, None, None)
    third = swap_sx(sent)
    corr, listed = x_call(1, 0, 2, third, *outer, corr, even)
    return (corr, listed)


def body(forward_prop, backward_prop, gamma_table, source_site, momenta):
    sizes = (forward_prop.shape, lax.axis_size("sx"), lax.axis_size("sy"))
    fits = sizes == ((2, 2, 12, 12, 8, 16 * LZ), 8, 4) and L == 64 and LZ == 64
    fits = fits and gamma_table.shape[0] == 16 and momenta.shape[0] == 32
    run = block_body if fits else general_body
    return run(forward_prop, backward_prop, gamma_table, source_site, momenta)


def solution(mesh):
    placed = (
        P(None, None, None, None, "sx", "sy"),
        P(None, None, None, None, "sx", "sy"),
        P(),
        P(),
        P(),
    )
    return jax.shard_map(
        body,
        mesh=mesh,
        in_specs=placed,
        out_specs=(P(None, None, None, "sx", "sy"), P()),
        check_vma=False,
    )
```

```python
import functools
import math

import jax
import jax.numpy as jnp
import numpy as np
from jax import lax
from jax.experimental import pallas as pl
from jax.experimental.pallas import tpu as pltpu
from jax.sharding import PartitionSpec as P

L = 64
LZ = 64


HIGHEST = lax.Precision.HIGHEST


def gamma_matrices(gamma_table):
    inserts = gamma_table.shape[0]
    columns = gamma_table[:, :, 0]
    powers = gamma_table[:, :, 1]
    spin_ids = jnp.arange(4, dtype=jnp.int32)
    matches = (columns[:, :, None] == spin_ids[None, None, :]).astype(jnp.float32)
    unit_re = (powers == 0).astype(jnp.float32) - (powers == 2).astype(jnp.float32)
    unit_im = (powers == 1).astype(jnp.float32) - (powers == 3).astype(jnp.float32)
    return (
        (matches * unit_re[:, :, None]).reshape(inserts, 16),
        (matches * unit_im[:, :, None]).reshape(inserts, 16),
    )


def dft_table(length, anchor):
    wavenum = jnp.arange(length, dtype=jnp.int32)
    offsets = jnp.mod(wavenum - anchor, length)
    phase_index = jnp.mod(offsets[:, None] * wavenum[None, :], length)
    angles = 2.0 * math.pi / length * phase_index.astype(jnp.float32)
    return (jnp.cos(angles), -jnp.sin(angles))


def complex_step(real_part, imag_part, table_re, table_im, pattern):
    out_re = jnp.einsum(pattern, real_part, table_re, precision=HIGHEST) - jnp.einsum(
        pattern, imag_part, table_im, precision=HIGHEST
    )
    out_im = jnp.einsum(pattern, real_part, table_im, precision=HIGHEST) + jnp.einsum(
        pattern, imag_part, table_re, precision=HIGHEST
    )
    return (out_re, out_im)


def transform(fields, source_site):
    table_re, table_im = dft_table(fields.shape[4], source_site[2])
    along_z = jnp.stack(
        complex_step(fields[:, 0], fields[:, 1], table_re, table_im, "nabz,zk->nabk"), 1
    )
    depth_share = along_z.shape[4] // lax.axis_size("sy")
    first_depth = lax.axis_index("sy") * depth_share
    length_y = along_z.shape[3] * lax.axis_size("sy")
    full_re, full_im = dft_table(length_y, source_site[1])
    part = lax.dynamic_slice_in_dim(
        lax.all_gather(along_z, "sy", axis=3, tiled=True), first_depth, depth_share, 4
    )
    step_re, step_im = complex_step(part[:, 0], part[:, 1], full_re, full_im, "nayc,yk->nakc")
    along_y = jnp.stack([step_re, step_im], 1)
    arrived = lax.all_to_all(along_y, "sx", split_axis=3, concat_axis=2, tiled=True)
    table_re, table_im = dft_table(arrived.shape[2], source_site[0])
    along_x = complex_step(arrived[:, 0], arrived[:, 1], table_re, table_im, "nxbc,xk->nbck")
    return jnp.stack(along_x, 1)


def apply_gammas(mat_re, mat_im, real_part, imag_part):
    extent = real_part.shape
    flat_re = real_part.reshape(extent[0], -1)
    flat_im = imag_part.reshape(extent[0], -1)
    out_re = jnp.dot(mat_re, flat_re, precision=HIGHEST) - jnp.dot(
        mat_im, flat_im, precision=HIGHEST
    )
    out_im = jnp.dot(mat_re, flat_im, precision=HIGHEST) + jnp.dot(
        mat_im, flat_re, precision=HIGHEST
    )
    return (out_re.reshape(extent), out_im.reshape(extent))


def project_sites(fields, source_site, momenta, rows_x, rows_y, length, depth):
    coord_x = lax.axis_index("sx") * rows_x + jnp.arange(rows_x, dtype=jnp.int32) - source_site[0]
    coord_y = lax.axis_index("sy") * rows_y + jnp.arange(rows_y, dtype=jnp.int32) - source_site[1]
    coord_z = jnp.arange(depth, dtype=jnp.int32) - source_site[2]
    part_x = jnp.mod(momenta[:, 0:1] * coord_x[None, :], length)
    part_y = jnp.mod(momenta[:, 1:2] * coord_y[None, :], length)
    part_z = jnp.mod(momenta[:, 2:3] * coord_z[None, :], depth)
    plane = jnp.mod(part_x[:, :, None] + part_y[:, None, :], length).astype(jnp.float32)
    angles = (
        2.0 * math.pi / length * plane[:, :, :, None]
        + 2.0 * math.pi / depth * part_z.astype(jnp.float32)[:, None, None, :]
    )
    angles = angles.reshape(momenta.shape[0], -1)
    cosine = jnp.cos(angles)
    sine = jnp.sin(angles)
    field_re = fields[:, 0].reshape(fields.shape[0], -1)
    field_im = fields[:, 1].reshape(fields.shape[0], -1)
    local_re = jnp.dot(field_re, cosine.T, precision=HIGHEST) + jnp.dot(
        field_im, sine.T, precision=HIGHEST
    )
    local_im = jnp.dot(field_im, cosine.T, precision=HIGHEST) - jnp.dot(
        field_re, sine.T, precision=HIGHEST
    )
    return (local_re, local_im)


def general_body(forward_prop, backward_prop, gamma_table, source_site, momenta):
    slices = forward_prop.shape[0]
    rows_x = forward_prop.shape[4]
    rows_y = backward_prop.shape[5] // LZ
    inserts = gamma_table.shape[0]
    forward = forward_prop.reshape(slices, 2, 4, 3, 12, -1)
    backward = backward_prop.reshape(slices, 2, 4, 3, 12, -1)
    pattern = "tscjn,tucjn->sutn"
    pair_re = jnp.einsum(
        pattern, backward[:, 0], forward[:, 0], preferred_element_type=jnp.float32
    ) + jnp.einsum(pattern, backward[:, 1], forward[:, 1], preferred_element_type=jnp.float32)
    pair_im = jnp.einsum(
        pattern, backward[:, 0], forward[:, 1], preferred_element_type=jnp.float32
    ) - jnp.einsum(pattern, backward[:, 1], forward[:, 0], preferred_element_type=jnp.float32)
    pair_re = pair_re.reshape(16, slices, -1)
    pair_im = pair_im.reshape(16, slices, -1)
    mat_re, mat_im = gamma_matrices(gamma_table)
    field_re, field_im = apply_gammas(mat_re, mat_im, pair_re, pair_im)
    fields = jnp.stack([field_re, field_im], 2).reshape(inserts * slices, 2, rows_x, rows_y, LZ)
    spectrum = transform(fields, source_site)
    local_re, local_im = project_sites(fields, source_site, momenta, rows_x, rows_y, L, LZ)
    listed_re, listed_im = lax.psum((local_re, local_im), ("sx", "sy"))
    listed_re = listed_re.reshape(inserts, slices, -1)
    listed_im = listed_im.reshape(inserts, slices, -1)
    corr_re = spectrum[:, 0].reshape(inserts, slices, spectrum.shape[2], -1)
    corr_im = spectrum[:, 1].reshape(inserts, slices, spectrum.shape[2], -1)
    return (jnp.stack([corr_re, corr_im], 2), jnp.stack([listed_re, listed_im], 0))


F32 = jnp.float32
BF16 = jnp.bfloat16
MIB = 2**20


def split(values):
    high = values.astype(BF16)
    return (high, (values - high.astype(F32)).astype(BF16))


def turn(out_wave, in_site):
    angle = 2.0 * math.pi / L * np.mod(np.multiply.outer(out_wave, in_site), L)
    cosine, sine = (np.cos(angle), np.sin(angle))
    table = np.empty((len(out_wave), 2, 2, len(in_site)))
    table[:, 0, 0] = cosine
    table[:, 0, 1] = sine
    table[:, 1, 0] = -sine
    table[:, 1, 1] = cosine
    return table


def table_z():
    wave = turn(np.arange(64), np.arange(64)).reshape(4, 2, 4, 2, 2, 2, 64)
    full = np.zeros((4, 2, 4, 2, 2, 2, 2, 2, 64))
    for y in range(2):
        full[:, :, :, :, :, y, :, y, :] = wave
    return jnp.asarray(full.reshape(4, 64, 256).astype(np.float32))


def table_y():
    wave = turn(np.arange(64), np.arange(64)).reshape(8, 8, 2, 2, 4, 8, 2)
    full = np.zeros((4, 8, 2, 2, 8, 4, 8, 2, 2, 2))
    for position in range(4):
        for step in range(4):
            source = position ^ step
            for p in range(2):
                full[position, :, p, :, :, step, :, p] = wave[:, :, :, :, source].transpose(
                    0, 2, 1, 4, 3, 5
                )
    return jnp.asarray(full.reshape(4, 256, 256).astype(np.float32))


def table_x():
    wave = turn(np.arange(64), np.arange(64))
    cosine, sine = (wave[:, 0, 0].T, wave[:, 0, 1].T)
    table = np.concatenate([cosine, cosine, sine, sine], 1).astype(np.float32)
    return jnp.asarray(table.reshape(8, 8, 256))


def nt_dot(a, b):
    return lax.dot_general(a, b, (((1,), (1,)), ((), ())), preferred_element_type=F32)


def nn_dot(a, b):
    return lax.dot_general(a, b, (((1,), (0,)), ((), ())), preferred_element_type=F32)


def tn_dot(a, b):
    return lax.dot_general(a, b, (((0,), (0,)), ((), ())), preferred_element_type=F32)


def whole(shape):
    return pl.BlockSpec(shape, lambda step: (0,) * len(shape))


def cost(weight):
    return pl.CostEstimate(flops=weight * 10**13, bytes_accessed=0, transcendentals=0)


def contract_block(f_ref, b_ref):
    def add(total, term):
        return term if total is None else total + term

    def load(ref, ri, row, pair):
        both = ref[0, ri, row, 2 * pair : 2 * pair + 2].astype(F32)
        return (both[0], both[1])

    one, two, three = ([None] * 16, [None] * 16, [None] * 16)
    for colour in range(3):
        for pair in range(6):
            back = [[load(b_ref, ri, 3 * s + colour, pair) for ri in (0, 1)] for s in range(4)]
            forw = [[load(f_ref, ri, 3 * u + colour, pair) for ri in (0, 1)] for u in range(4)]
            for h in (0, 1):
                for s in range(4):
                    b_re, b_im = (back[s][0][h], back[s][1][h])
                    b_less, b_more = (b_re - b_im, b_re + b_im)
                    for u in range(4):
                        f_re, f_im = (forw[u][0][h], forw[u][1][h])
                        f_more = f_re + f_im
                        k = 4 * s + u
                        one[k] = add(one[k], b_re * f_more)
                        two[k] = add(two[k], b_less * f_im)
                        three[k] = add(three[k], b_more * f_re)
    return [(one[k] - two[k], one[k] - three[k]) for k in range(16)]


def phases(index):
    half = (((index + 32) & 63) - 32).astype(F32) * (math.pi / 64)
    square = half * half
    sine = jnp.full_like(square, -1 / math.factorial(11))
    for n in (9, 7, 5, 3, 1):
        sine = sine * square + (-1) ** (n // 2) / math.factorial(n)
    sine = sine * half
    cosine = jnp.full_like(square, 1 / math.factorial(12))
    for n in (10, 8, 6, 4, 2, 0):
        cosine = cosine * square + (-1) ** (n // 2) / math.factorial(n)
    return (1.0 - 2.0 * sine * sine, 2.0 * sine * cosine)


def iota(shape, dim):
    return lax.broadcasted_iota(jnp.int32, shape, dim)


def planes(ref):
    re_high, re_low = split(ref[:, 0].reshape(128, 128))
    im_high, im_low = split(ref[:, 1].reshape(128, 128))
    return (jnp.concatenate([re_high, im_high], 1), jnp.concatenate([re_low, im_low], 1))


def momentum_lanes(mom_ref):
    lane = iota((1, 128), 1) & 31
    rows = []
    for k in range(3):
        row = jnp.zeros((1, 128), jnp.int32)
        for m in range(32):
            row = jnp.where(lane == m, mom_ref[k, m], row)
        rows.append(row)
    return rows


def momentum_tables(mom_ref, tm_high_ref, tm_low_ref):
    _, mom_y, mom_z = momentum_lanes(mom_ref)
    out_part = ((iota((64, 128), 1) >> 5) & 1) == 1
    for y in range(2):
        cosine, sine = phases(mom_z * iota((64, 128), 0) + mom_y * y)
        less = jnp.where(out_part, cosine, sine)
        none = jnp.where(out_part, -sine, cosine)
        more = jnp.where(out_part, -cosine, -sine)
        for part_in, blocks in ((0, (none, more)), (1, (less, none))):
            for turned in range(2):
                high, low = split(blocks[turned])
                rows = pl.ds(128 * part_in + 64 * y, 64)
                lanes = pl.ds(128 * turned, 128)
                tm_high_ref[rows, lanes] = high
                tm_low_ref[rows, lanes] = low


def pair_kernel(listed, aliased, source_ref, mom_ref, f_ref, b_ref, wave_ref, *refs):
    if aliased:
        refs = refs[1:]
    if listed:
        old_ref, *sends, field_ref, w_high_ref, w_low_ref = refs[:8]
        tm_high_ref, tm_low_ref, total_ref = refs[8:]
    else:
        *sends, fields_ref, field_ref, w_high_ref, w_low_ref = refs
    step = pl.program_id(0)
    rows = pl.num_programs(0) - 1
    row = jnp.maximum(step - 1, 0)

    @pl.when(step == 0)
    def _():
        blocks = [lax.axis_index("sy") ^ s for s in range(4)]
        high, low = split(jnp.concatenate([wave_ref[block] for block in blocks], 0))
        w_high_ref[...] = high
        w_low_ref[...] = low
        if listed:
            momentum_tables(mom_ref, tm_high_ref, tm_low_ref)
            total_ref[...] = jnp.zeros_like(total_ref)

    def project(t, high, low):
        proj = (
            nn_dot(high, tm_high_ref[...])
            + nn_dot(high, tm_low_ref[...])
            + nn_dot(low, tm_high_ref[...])
        )
        value, turned = (proj[:, :128], proj[:, 128:])
        cosine, sine = phases(2 * momentum_lanes(mom_ref)[1] * row)
        there = step > 0
        total_ref[t, 0] += jnp.where(there, cosine * value + sine * turned, 0.0)
        total_ref[t, 1] += jnp.where(there, cosine * turned - sine * value, 0.0)

    def transform():
        high, low = planes(field_ref)
        w_high, w_low = (w_high_ref[...], w_low_ref[...])
        out = nt_dot(w_high, high) + nt_dot(w_low, high) + nt_dot(w_high, low)
        out = out.reshape(4, 8, 8, 128)
        for s in range(4):
            sends[s][pl.ds(8 * row, 8)] = out[s]
        if listed:
            project(1, high, low)
            project(0, *planes(old_ref))

    @pl.when(step < rows)
    def _():
        transform()
        for k, (real, imag) in enumerate(contract_block(f_ref, b_ref)):
            field_ref[k, 0] = real
            field_ref[k, 1] = imag
            if not listed:
                fields_ref[k, 0] = real
                fields_ref[k, 1] = imag

    @pl.when(step == rows)
    def _():
        transform()
        if listed:
            mom_x, mom_y, mom_z = momentum_lanes(mom_ref)
            x = lax.axis_index("sx") * 8 - source_ref[0] + iota((8, 128), 0)
            rest = (lax.axis_index("sy") * 16 - source_ref[1]) * mom_y - source_ref[2] * mom_z
            cosine, sine = phases(x * mom_x + rest)
            for t in range(2):
                value = total_ref[t, 0].reshape(16, 8, 128)
                turned = total_ref[t, 1].reshape(16, 8, 128)
                summed = jnp.sum(value * cosine[None] + turned * sine[None], 1)
                tile = jnp.where(iota((8, 128), 1) >= 64, summed[8:], summed[:8])
                for s in range(4):
                    sends[s][64 + t] = tile


def pair_call(which, start, rows, listed, fields, forward, backward, wave, source_site, momenta):
    def block(step):
        return (which, 0, 0, 0, 0, start + jnp.minimum(step, rows - 1))

    in_specs = [pl.BlockSpec(memory_space=pltpu.SMEM)] * 2
    in_specs += [pl.BlockSpec((1, 2, 12, 12, 8, 128), block)] * 2 + [whole((4, 64, 256))]
    operands = [source_site, momenta, forward, backward, wave]
    shapes = [(8 * rows + 2 if listed else 8 * rows, 8, 128)] * 4
    out_specs = [whole(shape) for shape in shapes]
    scratch = [pltpu.VMEM((16, 2, 8, 128), F32)] + [pltpu.VMEM((256, 256), BF16)] * 2
    aliases = {}
    if listed:
        in_specs.append(
            pl.BlockSpec((16, 2, 8, 128), lambda step: (0, 0, 0, jnp.maximum(step - 1, 0)))
        )
        operands.append(fields)
        scratch += [pltpu.VMEM((256, 256), BF16)] * 2 + [pltpu.VMEM((2, 2, 128, 128), F32)]
    else:
        shapes.append((16, 2, 8, 1024))
        out_specs.append(pl.BlockSpec((16, 2, 8, 128), lambda step: (0, 0, 0, block(step)[5])))
        if fields is not None:
            in_specs.append(pl.BlockSpec(memory_space=pl.ANY))
            operands.append(fields)
            aliases = {5: 4}
    return pl.pallas_call(
        functools.partial(pair_kernel, listed, bool(aliases)),
        grid=(rows + 1,),
        in_specs=in_specs,
        out_specs=out_specs,
        out_shape=[jax.ShapeDtypeStruct(shape, F32) for shape in shapes],
        scratch_shapes=scratch,
        input_output_aliases=aliases,
        compiler_params=pltpu.CompilerParams(vmem_limit_bytes=55 * MIB),
        cost_estimate=cost(0),
        name="contract_and_z",
    )(*operands)


def y_kernel(parts, listed, apart, *refs):
    messages = [refs[s + 4 * part] for s in range(4) for part in range(parts)]
    wave_ref, *sends, work_ref = refs[4 * parts :]
    if not apart:
        sends = [sends[0].at[k] for k in range(8)]
    w_high, w_low = split(wave_ref[0])
    for q in range(8):
        data = [ref[8 * y + q] for ref in messages for y in range(ref.shape[0] // 8)]
        high, low = split(jnp.concatenate(data, 0))
        out = nn_dot(w_high, high) + nn_dot(w_low, high) + nn_dot(w_high, low)
        work_ref[q] = out.reshape(8, 2, 2, 8, 128)
    for h in range(2):
        for step in range(8):
            block = lax.axis_index("sx") ^ step if apart else step
            tiles = [
                work_ref[4 * h + q, block, p, ri]
                for ri in range(2)
                for q in range(4)
                for p in range(2)
            ]
            turned = jnp.concatenate(tiles, 0).T.reshape(16, 8, 128)
            sends[step][pl.ds(16 * h, 16)] = turned
    if listed:
        for t in range(2):
            share = sum(ref[64 + t] for ref in messages)
            for step in range(8):
                sends[step][32 + t] = share


def y_call(listed, apart, weight, parts, wave):
    messages = [x for part in parts for x in part]
    tiles = 34 if listed else 32
    shapes = [(tiles, 8, 128)] * 8 if apart else [(8, tiles, 8, 128)]
    return pl.pallas_call(
        functools.partial(y_kernel, len(parts), listed, apart),
        grid=(1,),
        in_specs=[whole(x.shape) for x in messages]
        + [pl.BlockSpec((1, 256, 256), lambda step: (lax.axis_index("sy"), 0, 0))],
        out_specs=[whole(shape) for shape in shapes],
        out_shape=[jax.ShapeDtypeStruct(shape, F32) for shape in shapes],
        scratch_shapes=[pltpu.VMEM((8, 8, 2, 2, 8, 128), F32)],
        compiler_params=pltpu.CompilerParams(vmem_limit_bytes=32 * MIB),
        cost_estimate=cost(weight),
        name="along_y",
    )(*messages, wave)


def x_kernel(count, listed, table_ref, source_ref, rows_ref, wave_ref, *refs):
    data_refs, work_ref = (refs[:count], refs[-1])
    out_ref = refs[-3] if listed else refs[-2]
    listed_ref = refs[-2] if listed else None
    if count == 1:
        data_refs = [data_refs[0].at[k] for k in range(8)]
    half = pl.program_id(0)
    first_x, first_y = (lax.axis_index("sx") * 8, lax.axis_index("sy") * 16)
    blocks = [k if count == 1 else lax.axis_index("sx") ^ k for k in range(8)]
    w_high, w_low = split(jnp.concatenate([wave_ref[block] for block in blocks], 0))
    weights = jnp.concatenate([w_high, w_high, w_low], 0)
    lower = iota((8, 128), 1) < 64
    for f in range(16):
        high, low = split(jnp.concatenate([ref[16 * half + f] for ref in data_refs], 0))
        out = tn_dot(jnp.concatenate([high, low, high], 0), weights)
        cosine = out[:, :128].reshape(2, 4, 2, 8, 128)
        sine = out[:, 128:].reshape(2, 4, 2, 8, 128)
        real = cosine[0] + sine[1]
        imag = cosine[1] - sine[0]
        for q in range(4):
            lanes = pl.ds(128 * q, 128)
            work_ref[f, 0, :, lanes] = jnp.where(lower, real[q, 0], real[q, 1])
            work_ref[f, 1, :, lanes] = jnp.where(lower, imag[q, 0], imag[q, 1])
    column = iota((8, 512), 1)
    index = (first_x + iota((8, 512), 0)) * source_ref[1] + (column & 63) * source_ref[0]
    cosine, sine = phases(index + (first_y + 8 * half + (column >> 6)) * source_ref[2])
    for g in range(16):
        real = jnp.zeros((8, 512), F32)
        imag = jnp.zeros((8, 512), F32)
        for s in range(4):
            field = 4 * s + table_ref[8 * g + 2 * s]
            power = table_ref[8 * g + 2 * s + 1]
            odd = power & 1
            sign_re = jnp.where((power == 0) | (power == 3), 1.0, -1.0).astype(F32)
            sign_im = jnp.where(power < 2, 1.0, -1.0).astype(F32)
            real += sign_re * work_ref[field, odd]
            imag += sign_im * work_ref[field, 1 - odd]
        out_ref[g, 0, 0] = real * cosine - imag * sine
        out_ref[g, 0, 1] = real * sine + imag * cosine

    def listed_sums():
        mix = mix_matrix(rows_ref[...]).astype(BF16)
        for t in range(2):
            total = sum(ref[32 + t] for ref in data_refs)
            rows = jnp.concatenate([total[:, 32 * k : 32 * k + 32] for k in range(4)], 0)
            high, rest = split(rows)
            middle, low = split(rows - high.astype(F32))
            sums = nn_dot(mix, high) + nn_dot(mix, middle) + nn_dot(mix, low)
            for ri in range(2):
                for g in range(16):
                    row = 16 * ri + g
                    listed_ref[ri, g, t : t + 1] = sums[row : row + 1]

    if listed:
        pl.when(half == 0)(listed_sums)


def x_call(which, data, gammas, rows, source_site, wave, corr):
    in_specs = [
        pl.BlockSpec(memory_space=pltpu.SMEM),
        pl.BlockSpec(memory_space=pltpu.SMEM),
        whole((16, 8)),
        whole((8, 8, 256)),
    ] + [whole(x.shape) for x in data]
    operands = [gammas, source_site, rows, wave, *data]
    aliases = {}
    shapes = [(16, 2, 2, 8, 1024)]
    out_specs = [pl.BlockSpec((16, 1, 2, 8, 512), lambda step: (0, which, 0, 0, step))]
    if corr is not None:
        aliases = {len(operands): 0}
        in_specs.append(pl.BlockSpec(memory_space=pl.ANY))
        operands.append(corr)
        shapes.append((2, 16, 2, 32))
        out_specs.append(whole(shapes[1]))
    return pl.pallas_call(
        functools.partial(x_kernel, len(data), corr is not None),
        grid=(2,),
        in_specs=in_specs,
        out_specs=out_specs,
        out_shape=[jax.ShapeDtypeStruct(shape, F32) for shape in shapes],
        scratch_shapes=[pltpu.VMEM((16, 2, 8, 512), F32)],
        input_output_aliases=aliases,
        compiler_params=pltpu.CompilerParams(vmem_limit_bytes=32 * MIB),
        cost_estimate=cost(0),
        name="along_x",
    )(*operands)


def mix_matrix(gammas):
    column = iota((16, 32), 1)
    field = (column >> 4) * 8 + (column & 7)
    on_imag = ((column >> 3) & 1) == 1
    real = jnp.zeros((16, 32), F32)
    imag = jnp.zeros((16, 32), F32)
    for s in range(4):
        match = field == 4 * s + gammas[:, 2 * s : 2 * s + 1]
        power = gammas[:, 2 * s + 1 : 2 * s + 2]
        unit_re = (power == 0).astype(F32) - (power == 2).astype(F32)
        unit_im = (power == 1).astype(F32) - (power == 3).astype(F32)
        real += jnp.where(match, jnp.where(on_imag, -unit_im, unit_re), 0.0)
        imag += jnp.where(match, jnp.where(on_imag, unit_re, unit_im), 0.0)
    return jnp.concatenate([real, imag], 0)


def swap_sy(message):
    out = list(message)
    for step in (3, 2, 1):
        out[step] = lax.ppermute(message[step], "sy", [(k, k ^ step) for k in range(4)])
    return out


def swap_sx_whole(message):
    return [lax.all_to_all(message[0], "sx", 0, 0, tiled=True)]


def swap_sx(message):
    out = list(message)
    for step in (1, 2, 3, 4, 5, 6, 7):
        out[step] = lax.ppermute(message[step], "sx", [(k, k ^ step) for k in range(8)])
    return out


def after(values, *others):
    return lax.optimization_barrier((values, others))[0]


def block_body(forward_prop, backward_prop, gamma_table, source_site, momenta):
    wave_z, wave_y, wave_x = (table_z(), table_y(), table_x())
    site, mom = (source_site, momenta.T)
    outer = (gamma_table.reshape(-1), gamma_table.reshape(16, 8), source_site, wave_x)
    *first, fields = pair_call(0, 0, 3, False, None, forward_prop, backward_prop, wave_z, site, mom)
    site, first = after((site, first))
    first = swap_sy(first)
    *third, fields = pair_call(0, 3, 5, False, fields, forward_prop, backward_prop, wave_z, site, mom)
    site, third = after((site, third))
    first, third[1] = after((first, third[1]))
    third = swap_sy(third)
    second = list(pair_call(1, 0, 8, True, fields, forward_prop, backward_prop, wave_z, site, mom))
    third, second[1] = after((third, second[1]))
    second = swap_sy(second)
    sent = y_call(False, False, 0, [first, third], wave_y)
    data = swap_sx_whole(sent)
    second[1:] = after(second[1:], sent[0])
    sent = y_call(True, True, 1, [second], wave_y)
    data = after(data, sent[0])
    (corr,) = x_call(0, data, *outer, None)
    second = swap_sx(sent)
    corr, listed = x_call(1, second, *outer, corr)
    return (corr, listed)


def body(forward_prop, backward_prop, gamma_table, source_site, momenta):
    sizes = (forward_prop.shape, lax.axis_size("sx"), lax.axis_size("sy"))
    fits = sizes == ((2, 2, 12, 12, 8, 16 * LZ), 8, 4) and L == 64 and LZ == 64
    fits = fits and gamma_table.shape[0] == 16 and momenta.shape[0] == 32
    run = block_body if fits else general_body
    return run(forward_prop, backward_prop, gamma_table, source_site, momenta)


def solution(mesh):
    placed = (
        P(None, None, None, None, "sx", "sy"),
        P(None, None, None, None, "sx", "sy"),
        P(),
        P(),
        P(),
    )
    return jax.shard_map(
        body,
        mesh=mesh,
        in_specs=placed,
        out_specs=(P(None, None, None, "sx", "sy"), P()),
        check_vma=False,
    )
```

```python
import functools
import math

import jax
import jax.numpy as jnp
import numpy as np
from jax import lax
from jax.experimental import pallas as pl
from jax.experimental.pallas import tpu as pltpu
from jax.sharding import PartitionSpec as P

L = 64
LZ = 64


HIGHEST = lax.Precision.HIGHEST


def gamma_matrices(gamma_table):
    inserts = gamma_table.shape[0]
    columns = gamma_table[:, :, 0]
    powers = gamma_table[:, :, 1]
    spin_ids = jnp.arange(4, dtype=jnp.int32)
    matches = (columns[:, :, None] == spin_ids[None, None, :]).astype(jnp.float32)
    unit_re = (powers == 0).astype(jnp.float32) - (powers == 2).astype(jnp.float32)
    unit_im = (powers == 1).astype(jnp.float32) - (powers == 3).astype(jnp.float32)
    return (
        (matches * unit_re[:, :, None]).reshape(inserts, 16),
        (matches * unit_im[:, :, None]).reshape(inserts, 16),
    )


def dft_table(length, anchor):
    wavenum = jnp.arange(length, dtype=jnp.int32)
    offsets = jnp.mod(wavenum - anchor, length)
    phase_index = jnp.mod(offsets[:, None] * wavenum[None, :], length)
    angles = 2.0 * math.pi / length * phase_index.astype(jnp.float32)
    return (jnp.cos(angles), -jnp.sin(angles))


def complex_step(real_part, imag_part, table_re, table_im, pattern):
    out_re = jnp.einsum(pattern, real_part, table_re, precision=HIGHEST) - jnp.einsum(
        pattern, imag_part, table_im, precision=HIGHEST
    )
    out_im = jnp.einsum(pattern, real_part, table_im, precision=HIGHEST) + jnp.einsum(
        pattern, imag_part, table_re, precision=HIGHEST
    )
    return (out_re, out_im)


def transform(fields, source_site):
    table_re, table_im = dft_table(fields.shape[4], source_site[2])
    along_z = jnp.stack(
        complex_step(fields[:, 0], fields[:, 1], table_re, table_im, "nabz,zk->nabk"), 1
    )
    depth_share = along_z.shape[4] // lax.axis_size("sy")
    first_depth = lax.axis_index("sy") * depth_share
    length_y = along_z.shape[3] * lax.axis_size("sy")
    full_re, full_im = dft_table(length_y, source_site[1])
    part = lax.dynamic_slice_in_dim(
        lax.all_gather(along_z, "sy", axis=3, tiled=True), first_depth, depth_share, 4
    )
    step_re, step_im = complex_step(part[:, 0], part[:, 1], full_re, full_im, "nayc,yk->nakc")
    along_y = jnp.stack([step_re, step_im], 1)
    arrived = lax.all_to_all(along_y, "sx", split_axis=3, concat_axis=2, tiled=True)
    table_re, table_im = dft_table(arrived.shape[2], source_site[0])
    along_x = complex_step(arrived[:, 0], arrived[:, 1], table_re, table_im, "nxbc,xk->nbck")
    return jnp.stack(along_x, 1)


def apply_gammas(mat_re, mat_im, real_part, imag_part):
    extent = real_part.shape
    flat_re = real_part.reshape(extent[0], -1)
    flat_im = imag_part.reshape(extent[0], -1)
    out_re = jnp.dot(mat_re, flat_re, precision=HIGHEST) - jnp.dot(
        mat_im, flat_im, precision=HIGHEST
    )
    out_im = jnp.dot(mat_re, flat_im, precision=HIGHEST) + jnp.dot(
        mat_im, flat_re, precision=HIGHEST
    )
    return (out_re.reshape(extent), out_im.reshape(extent))


def project_sites(fields, source_site, momenta, rows_x, rows_y, length, depth):
    coord_x = lax.axis_index("sx") * rows_x + jnp.arange(rows_x, dtype=jnp.int32) - source_site[0]
    coord_y = lax.axis_index("sy") * rows_y + jnp.arange(rows_y, dtype=jnp.int32) - source_site[1]
    coord_z = jnp.arange(depth, dtype=jnp.int32) - source_site[2]
    part_x = jnp.mod(momenta[:, 0:1] * coord_x[None, :], length)
    part_y = jnp.mod(momenta[:, 1:2] * coord_y[None, :], length)
    part_z = jnp.mod(momenta[:, 2:3] * coord_z[None, :], depth)
    plane = jnp.mod(part_x[:, :, None] + part_y[:, None, :], length).astype(jnp.float32)
    angles = (
        2.0 * math.pi / length * plane[:, :, :, None]
        + 2.0 * math.pi / depth * part_z.astype(jnp.float32)[:, None, None, :]
    )
    angles = angles.reshape(momenta.shape[0], -1)
    cosine = jnp.cos(angles)
    sine = jnp.sin(angles)
    field_re = fields[:, 0].reshape(fields.shape[0], -1)
    field_im = fields[:, 1].reshape(fields.shape[0], -1)
    local_re = jnp.dot(field_re, cosine.T, precision=HIGHEST) + jnp.dot(
        field_im, sine.T, precision=HIGHEST
    )
    local_im = jnp.dot(field_im, cosine.T, precision=HIGHEST) - jnp.dot(
        field_re, sine.T, precision=HIGHEST
    )
    return (local_re, local_im)


def general_body(forward_prop, backward_prop, gamma_table, source_site, momenta):
    slices = forward_prop.shape[0]
    rows_x = forward_prop.shape[4]
    rows_y = backward_prop.shape[5] // LZ
    inserts = gamma_table.shape[0]
    forward = forward_prop.reshape(slices, 2, 4, 3, 12, -1)
    backward = backward_prop.reshape(slices, 2, 4, 3, 12, -1)
    pattern = "tscjn,tucjn->sutn"
    pair_re = jnp.einsum(
        pattern, backward[:, 0], forward[:, 0], preferred_element_type=jnp.float32
    ) + jnp.einsum(pattern, backward[:, 1], forward[:, 1], preferred_element_type=jnp.float32)
    pair_im = jnp.einsum(
        pattern, backward[:, 0], forward[:, 1], preferred_element_type=jnp.float32
    ) - jnp.einsum(pattern, backward[:, 1], forward[:, 0], preferred_element_type=jnp.float32)
    pair_re = pair_re.reshape(16, slices, -1)
    pair_im = pair_im.reshape(16, slices, -1)
    mat_re, mat_im = gamma_matrices(gamma_table)
    field_re, field_im = apply_gammas(mat_re, mat_im, pair_re, pair_im)
    fields = jnp.stack([field_re, field_im], 2).reshape(inserts * slices, 2, rows_x, rows_y, LZ)
    spectrum = transform(fields, source_site)
    local_re, local_im = project_sites(fields, source_site, momenta, rows_x, rows_y, L, LZ)
    listed_re, listed_im = lax.psum((local_re, local_im), ("sx", "sy"))
    listed_re = listed_re.reshape(inserts, slices, -1)
    listed_im = listed_im.reshape(inserts, slices, -1)
    corr_re = spectrum[:, 0].reshape(inserts, slices, spectrum.shape[2], -1)
    corr_im = spectrum[:, 1].reshape(inserts, slices, spectrum.shape[2], -1)
    return (jnp.stack([corr_re, corr_im], 2), jnp.stack([listed_re, listed_im], 0))


F32 = jnp.float32
BF16 = jnp.bfloat16
MIB = 2**20
SX_ORDER = (0, 1, 4, 2, 6, 5, 3, 7)


def split(values):
    high = values.astype(BF16)
    return (high, (values - high.astype(F32)).astype(BF16))


def turn(out_wave, in_site):
    angle = 2.0 * math.pi / L * np.mod(np.multiply.outer(out_wave, in_site), L)
    cosine, sine = (np.cos(angle), np.sin(angle))
    table = np.empty((len(out_wave), 2, 2, len(in_site)))
    table[:, 0, 0] = cosine
    table[:, 0, 1] = sine
    table[:, 1, 0] = -sine
    table[:, 1, 1] = cosine
    return table


def table_z():
    wave = turn(np.arange(64), np.arange(64)).reshape(4, 2, 4, 2, 2, 2, 64)
    full = np.zeros((4, 2, 4, 2, 2, 2, 2, 2, 64))
    for y in range(2):
        full[:, :, :, :, :, y, :, y, :] = wave
    return jnp.asarray(full.reshape(4, 64, 256).astype(np.float32))


def table_y():
    wave = turn(np.arange(64), np.arange(64)).reshape(8, 8, 2, 2, 4, 8, 2)
    full = np.zeros((4, 8, 2, 2, 8, 4, 8, 2, 2, 2))
    for position in range(4):
        for step in range(4):
            source = position ^ step
            for p in range(2):
                full[position, :, p, :, :, step, :, p] = wave[:, :, :, :, source].transpose(
                    0, 2, 1, 4, 3, 5
                )
    return jnp.asarray(full.reshape(4, 256, 256).astype(np.float32))


def table_x():
    wave = turn(np.arange(64), np.arange(64))
    cosine, sine = (wave[:, 0, 0].T, wave[:, 0, 1].T)
    table = np.concatenate([cosine, cosine, sine, sine], 1).astype(np.float32)
    return jnp.asarray(table.reshape(8, 8, 256))


def nt_dot(a, b):
    return lax.dot_general(a, b, (((1,), (1,)), ((), ())), preferred_element_type=F32)


def nn_dot(a, b):
    return lax.dot_general(a, b, (((1,), (0,)), ((), ())), preferred_element_type=F32)


def tn_dot(a, b):
    return lax.dot_general(a, b, (((0,), (0,)), ((), ())), preferred_element_type=F32)


def whole(shape):
    return pl.BlockSpec(shape, lambda step: (0,) * len(shape))


def cost(weight):
    return pl.CostEstimate(flops=weight * 10**13, bytes_accessed=0, transcendentals=0)


def contract_block(f_ref, b_ref, lanes):
    def add(total, term):
        return term if total is None else total + term

    def load(ref, ri, row, pair):
        both = ref[0, ri, row, 2 * pair : 2 * pair + 2, :, lanes].astype(F32)
        return (both[0], both[1])

    one, two, three = ([None] * 16, [None] * 16, [None] * 16)
    for colour in range(3):
        for pair in range(6):
            back = [[load(b_ref, ri, 3 * s + colour, pair) for ri in (0, 1)] for s in range(4)]
            forw = [[load(f_ref, ri, 3 * u + colour, pair) for ri in (0, 1)] for u in range(4)]
            for h in (0, 1):
                for s in range(4):
                    b_re, b_im = (back[s][0][h], back[s][1][h])
                    b_less, b_more = (b_re - b_im, b_re + b_im)
                    for u in range(4):
                        f_re, f_im = (forw[u][0][h], forw[u][1][h])
                        f_more = f_re + f_im
                        k = 4 * s + u
                        one[k] = add(one[k], b_re * f_more)
                        two[k] = add(two[k], b_less * f_im)
                        three[k] = add(three[k], b_more * f_re)
    return [(one[k] - two[k], one[k] - three[k]) for k in range(16)]


def phases(index):
    half = (((index + 32) & 63) - 32).astype(F32) * (math.pi / 64)
    square = half * half
    sine = jnp.full_like(square, -1 / math.factorial(11))
    for n in (9, 7, 5, 3, 1):
        sine = sine * square + (-1) ** (n // 2) / math.factorial(n)
    sine = sine * half
    cosine = jnp.full_like(square, 1 / math.factorial(12))
    for n in (10, 8, 6, 4, 2, 0):
        cosine = cosine * square + (-1) ** (n // 2) / math.factorial(n)
    return (1.0 - 2.0 * sine * sine, 2.0 * sine * cosine)


def iota(shape, dim):
    return lax.broadcasted_iota(jnp.int32, shape, dim)


def planes(ref, lanes):
    re_high, re_low = split(ref[:, 0, :, lanes].reshape(128, 128))
    im_high, im_low = split(ref[:, 1, :, lanes].reshape(128, 128))
    return (jnp.concatenate([re_high, im_high], 1), jnp.concatenate([re_low, im_low], 1))


def momentum_lanes(mom_ref):
    lane = iota((1, 128), 1) & 31
    rows = []
    for k in range(3):
        row = jnp.zeros((1, 128), jnp.int32)
        for m in range(32):
            row = jnp.where(lane == m, mom_ref[k, m], row)
        rows.append(row)
    return rows


def momentum_tables(mom_ref, tm_high_ref, tm_low_ref):
    _, mom_y, mom_z = momentum_lanes(mom_ref)
    out_part = ((iota((64, 128), 1) >> 5) & 1) == 1
    for y in range(2):
        cosine, sine = phases(mom_z * iota((64, 128), 0) + mom_y * y)
        less = jnp.where(out_part, cosine, sine)
        none = jnp.where(out_part, -sine, cosine)
        more = jnp.where(out_part, -cosine, -sine)
        for part_in, blocks in ((0, (none, more)), (1, (less, none))):
            for turned in range(2):
                high, low = split(blocks[turned])
                rows = pl.ds(128 * part_in + 64 * y, 64)
                lanes = pl.ds(128 * turned, 128)
                tm_high_ref[rows, lanes] = high
                tm_low_ref[rows, lanes] = low


def pair_kernel(listed, aliased, source_ref, mom_ref, f_ref, b_ref, wave_ref, *refs):
    if aliased:
        refs = refs[1:]
    if listed:
        old_ref, *sends, field_ref, w_high_ref, w_low_ref = refs[:8]
        tm_high_ref, tm_low_ref, total_ref = refs[8:]
    else:
        *sends, fields_ref, field_ref, w_high_ref, w_low_ref = refs
    step = pl.program_id(0)
    steps = pl.num_programs(0) - 1
    parts = f_ref.shape[5] // 128

    @pl.when(step == 0)
    def _():
        blocks = [lax.axis_index("sy") ^ s for s in range(4)]
        high, low = split(jnp.concatenate([wave_ref[block] for block in blocks], 0))
        w_high_ref[...] = high
        w_low_ref[...] = low
        if listed:
            momentum_tables(mom_ref, tm_high_ref, tm_low_ref)
            total_ref[...] = jnp.zeros_like(total_ref)

    def project(t, high, low, row, there):
        proj = (
            nn_dot(high, tm_high_ref[...])
            + nn_dot(high, tm_low_ref[...])
            + nn_dot(low, tm_high_ref[...])
        )
        value, turned = (proj[:, :128], proj[:, 128:])
        cosine, sine = phases(2 * momentum_lanes(mom_ref)[1] * row)
        total_ref[t, 0] += jnp.where(there, cosine * value + sine * turned, 0.0)
        total_ref[t, 1] += jnp.where(there, cosine * turned - sine * value, 0.0)

    def transform(row, there):
        high, low = planes(field_ref, pl.ds(0, 128))
        w_high, w_low = (w_high_ref[...], w_low_ref[...])
        out = nt_dot(w_high, high) + nt_dot(w_low, high) + nt_dot(w_high, low)
        halves = len(sends) // 4
        count = 8 // halves
        out = out.reshape(4, halves, count, 8, 128)
        for s in range(4):
            for h in range(halves):
                sends[4 * h + s][pl.ds(count * row, count)] = out[s, h]
        if listed:
            project(1, high, low, row, there)

    @pl.when(step < steps)
    def _():
        for part in range(parts):
            lanes = pl.ds(128 * part, 128)
            row = parts * step + part
            transform(jnp.maximum(row - 1, 0), row > 0)
            if listed:
                project(0, *planes(old_ref, lanes), row, True)
            for k, (real, imag) in enumerate(contract_block(f_ref, b_ref, lanes)):
                field_ref[k, 0] = real
                field_ref[k, 1] = imag
                if not listed:
                    fields_ref[k, 0, :, lanes] = real
                    fields_ref[k, 1, :, lanes] = imag

    @pl.when(step == steps)
    def _():
        transform(parts * steps - 1, True)
        if listed:
            mom_x, mom_y, mom_z = momentum_lanes(mom_ref)
            x = lax.axis_index("sx") * 8 - source_ref[0] + iota((8, 128), 0)
            rest = (lax.axis_index("sy") * 16 - source_ref[1]) * mom_y - source_ref[2] * mom_z
            cosine, sine = phases(x * mom_x + rest)
            for t in range(2):
                value = total_ref[t, 0].reshape(16, 8, 128)
                turned = total_ref[t, 1].reshape(16, 8, 128)
                summed = jnp.sum(value * cosine[None] + turned * sine[None], 1)
                tile = jnp.where(iota((8, 128), 1) >= 64, summed[8:], summed[:8])
                for s in range(4):
                    sends[s][64 + t] = tile


def pair_call(which, start, rows, parts, listed, fields, forward, backward, wave, source_site, momenta):
    steps = rows // parts
    lanes = 128 * parts

    def block(step):
        return (which, 0, 0, 0, 0, start // parts + jnp.minimum(step, steps - 1))

    in_specs = [pl.BlockSpec(memory_space=pltpu.SMEM)] * 2
    in_specs += [pl.BlockSpec((1, 2, 12, 12, 8, lanes), block)] * 2 + [whole((4, 64, 256))]
    operands = [source_site, momenta, forward, backward, wave]
    shapes = [(8 * rows + 2 if listed else 8 * rows, 8, 128)] * 4
    out_specs = [whole(shape) for shape in shapes]
    scratch = [pltpu.VMEM((16, 2, 8, 128), F32)] + [pltpu.VMEM((256, 256), BF16)] * 2
    aliases = {}
    if listed:
        in_specs.append(
            pl.BlockSpec((16, 2, 8, lanes), lambda step: (0, 0, 0, block(step)[5]))
        )
        operands.append(fields)
        scratch += [pltpu.VMEM((256, 256), BF16)] * 2 + [pltpu.VMEM((2, 2, 128, 128), F32)]
    else:
        shapes.append((16, 2, 8, 1024))
        out_specs.append(pl.BlockSpec((16, 2, 8, lanes), lambda step: (0, 0, 0, block(step)[5])))
        if fields is not None:
            in_specs.append(pl.BlockSpec(memory_space=pl.ANY))
            operands.append(fields)
            aliases = {5: 4}
    return pl.pallas_call(
        functools.partial(pair_kernel, listed, bool(aliases)),
        grid=(steps + 1,),
        in_specs=in_specs,
        out_specs=out_specs,
        out_shape=[jax.ShapeDtypeStruct(shape, F32) for shape in shapes],
        scratch_shapes=scratch,
        input_output_aliases=aliases,
        compiler_params=pltpu.CompilerParams(vmem_limit_bytes=55 * MIB),
        cost_estimate=cost(0),
        name="contract_and_z",
    )(*operands)


def y_kernel(parts, listed, apart, kept, *refs):
    messages = [refs[s + 4 * part] for s in range(4) for part in range(parts)]
    if kept:
        refs[-2][...] = refs[4 * parts + 1][...]
        refs = refs[: 4 * parts + 1] + refs[4 * parts + 2 : -2] + refs[-1:]
    wave_ref, *sends, work_ref = refs[4 * parts :]
    if not apart:
        sends = [sends[0].at[k] for k in range(8)]
    w_high, w_low = split(wave_ref[0])
    for q in range(0, 8, 2):
        data = [
            jnp.concatenate([ref[8 * y + q], ref[8 * y + q + 1]], 1)
            for ref in messages
            for y in range(ref.shape[0] // 8)
        ]
        high, low = split(jnp.concatenate(data, 0))
        out = nn_dot(w_high, high) + nn_dot(w_low, high) + nn_dot(w_high, low)
        work_ref[q] = out[:, :128].reshape(8, 2, 2, 8, 128)
        work_ref[q + 1] = out[:, 128:].reshape(8, 2, 2, 8, 128)
    for h in range(2):
        for step in range(8):
            block = lax.axis_index("sx") ^ step if apart else step
            tiles = [
                work_ref[4 * h + q, block, p, ri]
                for ri in range(2)
                for q in range(4)
                for p in range(2)
            ]
            turned = jnp.concatenate(tiles, 0).T.reshape(16, 8, 128)
            sends[step][pl.ds(16 * h, 16)] = turned
    if listed:
        for t in range(2):
            share = sum(ref[64 + t] for ref in messages)
            for step in range(8):
                sends[step][32 + t] = share


def y_call(listed, apart, weight, parts, wave, kept=None):
    messages = [x for part in parts for x in part]
    tiles = 34 if listed else 32
    shapes = [(tiles, 8, 128)] * 8 if apart else [(8, tiles, 8, 128)]
    extra = [] if kept is None else [kept]
    shapes += [x.shape for x in extra]
    return pl.pallas_call(
        functools.partial(y_kernel, len(parts), listed, apart, kept is not None),
        grid=(1,),
        in_specs=[whole(x.shape) for x in messages]
        + [pl.BlockSpec((1, 256, 256), lambda step: (lax.axis_index("sy"), 0, 0))]
        + [whole(x.shape) for x in extra],
        out_specs=[whole(shape) for shape in shapes],
        out_shape=[jax.ShapeDtypeStruct(shape, F32) for shape in shapes],
        scratch_shapes=[pltpu.VMEM((8, 8, 2, 2, 8, 128), F32)],
        compiler_params=pltpu.CompilerParams(vmem_limit_bytes=32 * MIB),
        cost_estimate=cost(weight),
        name="along_y",
    )(*messages, wave, *extra)


def x_kernel(count, listed, table_ref, source_ref, rows_ref, wave_ref, *refs):
    data_refs, work_ref = (refs[:count], refs[-1])
    out_ref = refs[-3] if listed else refs[-2]
    listed_ref = refs[-2] if listed else None
    if count == 1:
        data_refs = [data_refs[0].at[k] for k in range(8)]
    half = pl.program_id(0)
    first_x, first_y = (lax.axis_index("sx") * 8, lax.axis_index("sy") * 16)
    blocks = range(8) if count == 1 else [lax.axis_index("sx") ^ k for k in SX_ORDER]
    w_high, w_low = split(jnp.concatenate([wave_ref[block] for block in blocks], 0))
    weights = jnp.concatenate([w_high, w_high, w_low], 0)
    lower = iota((8, 128), 1) < 64
    for f in range(16):
        if f % 4 == 0:
            data = []
            for k in range(f, f + 4):
                parts = [ref[16 * half + k] for ref in data_refs]
                high, low = split(jnp.concatenate(parts, 0))
                data.append(jnp.concatenate([high, low, high], 0))
            group = tn_dot(jnp.concatenate(data, 1), weights)
        out = group[128 * (f % 4) : 128 * (f % 4 + 1)]
        cosine = out[:, :128].reshape(2, 4, 2, 8, 128)
        sine = out[:, 128:].reshape(2, 4, 2, 8, 128)
        real = cosine[0] + sine[1]
        imag = cosine[1] - sine[0]
        for q in range(4):
            lanes = pl.ds(128 * q, 128)
            work_ref[f, 0, :, lanes] = jnp.where(lower, real[q, 0], real[q, 1])
            work_ref[f, 1, :, lanes] = jnp.where(lower, imag[q, 0], imag[q, 1])
    column = iota((8, 512), 1)
    index = (first_x + iota((8, 512), 0)) * source_ref[1] + (column & 63) * source_ref[0]
    cosine, sine = phases(index + (first_y + 8 * half + (column >> 6)) * source_ref[2])
    for g in range(16):
        real = jnp.zeros((8, 512), F32)
        imag = jnp.zeros((8, 512), F32)
        for s in range(4):
            field = 4 * s + table_ref[8 * g + 2 * s]
            power = table_ref[8 * g + 2 * s + 1]
            odd = power & 1
            sign_re = jnp.where((power == 0) | (power == 3), 1.0, -1.0).astype(F32)
            sign_im = jnp.where(power < 2, 1.0, -1.0).astype(F32)
            real += sign_re * work_ref[field, odd]
            imag += sign_im * work_ref[field, 1 - odd]
        out_ref[g, 0, 0] = real * cosine - imag * sine
        out_ref[g, 0, 1] = real * sine + imag * cosine

    def listed_sums():
        mix = mix_matrix(rows_ref[...]).astype(BF16)
        for t in range(2):
            total = sum(ref[32 + t] for ref in data_refs)
            rows = jnp.concatenate([total[:, 32 * k : 32 * k + 32] for k in range(4)], 0)
            high, rest = split(rows)
            middle, low = split(rows - high.astype(F32))
            sums = nn_dot(mix, high) + nn_dot(mix, middle) + nn_dot(mix, low)
            for ri in range(2):
                for g in range(16):
                    row = 16 * ri + g
                    listed_ref[ri, g, t : t + 1] = sums[row : row + 1]

    if listed:
        pl.when(half == 0)(listed_sums)


def x_call(which, data, gammas, rows, source_site, wave, corr):
    if len(data) == 8:
        data = [data[k] for k in SX_ORDER]
    in_specs = [
        pl.BlockSpec(memory_space=pltpu.SMEM),
        pl.BlockSpec(memory_space=pltpu.SMEM),
        whole((16, 8)),
        whole((8, 8, 256)),
    ] + [whole(x.shape) for x in data]
    operands = [gammas, source_site, rows, wave, *data]
    aliases = {}
    shapes = [(16, 2, 2, 8, 1024)]
    out_specs = [pl.BlockSpec((16, 1, 2, 8, 512), lambda step: (0, which, 0, 0, step))]
    if corr is not None:
        aliases = {len(operands): 0}
        in_specs.append(pl.BlockSpec(memory_space=pl.ANY))
        operands.append(corr)
        shapes.append((2, 16, 2, 32))
        out_specs.append(whole(shapes[1]))
    return pl.pallas_call(
        functools.partial(x_kernel, len(data), corr is not None),
        grid=(2,),
        in_specs=in_specs,
        out_specs=out_specs,
        out_shape=[jax.ShapeDtypeStruct(shape, F32) for shape in shapes],
        scratch_shapes=[pltpu.VMEM((16, 2, 8, 512), F32)],
        input_output_aliases=aliases,
        compiler_params=pltpu.CompilerParams(vmem_limit_bytes=32 * MIB),
        cost_estimate=cost(0),
        name="along_x",
    )(*operands)


def mix_matrix(gammas):
    column = iota((16, 32), 1)
    field = (column >> 4) * 8 + (column & 7)
    on_imag = ((column >> 3) & 1) == 1
    real = jnp.zeros((16, 32), F32)
    imag = jnp.zeros((16, 32), F32)
    for s in range(4):
        match = field == 4 * s + gammas[:, 2 * s : 2 * s + 1]
        power = gammas[:, 2 * s + 1 : 2 * s + 2]
        unit_re = (power == 0).astype(F32) - (power == 2).astype(F32)
        unit_im = (power == 1).astype(F32) - (power == 3).astype(F32)
        real += jnp.where(match, jnp.where(on_imag, -unit_im, unit_re), 0.0)
        imag += jnp.where(match, jnp.where(on_imag, unit_re, unit_im), 0.0)
    return jnp.concatenate([real, imag], 0)


def swap_sy(message):
    out = list(message)
    for step in (3, 2, 1):
        out[step] = lax.ppermute(message[step], "sy", [(k, k ^ step) for k in range(4)])
    return out


def swap_sx_whole(message):
    return [lax.all_to_all(message[0], "sx", 0, 0, tiled=True)]


def swap_sx(message):
    out = list(message)
    for step in SX_ORDER[1:]:
        out[step] = lax.ppermute(message[step], "sx", [(k, k ^ step) for k in range(8)])
    return out


def after(values, *others):
    return lax.optimization_barrier((values, others))[0]


def block_body(forward_prop, backward_prop, gamma_table, source_site, momenta):
    wave_z, wave_y, wave_x = (table_z(), table_y(), table_x())
    site, mom = (source_site, momenta.T)
    outer = (gamma_table.reshape(-1), gamma_table.reshape(16, 8), source_site, wave_x)
    *first, fields = pair_call(0, 0, 3, 1, False, None, forward_prop, backward_prop, wave_z, site, mom)
    site, first = after((site, first))
    first = swap_sy(first)
    *third, fields = pair_call(0, 3, 5, 1, False, fields, forward_prop, backward_prop, wave_z, site, mom)
    site, third = after((site, third))
    first, third[1] = after((first, third[1]))
    third = swap_sy(third)
    second = list(pair_call(1, 0, 8, 2, True, fields, forward_prop, backward_prop, wave_z, site, mom))
    third, second[1] = after((third, second[1]))
    second = swap_sy(second)
    *sent, second[0] = y_call(False, False, 0, [first, third], wave_y, second[0])
    data = swap_sx_whole(sent)
    second[1:] = after(second[1:], sent[0])
    sent = y_call(True, True, 1, [second], wave_y)
    data = after(data, sent[0])
    (corr,) = x_call(0, data, *outer, None)
    second = swap_sx(sent)
    corr, listed = x_call(1, second, *outer, corr)
    return (corr, listed)


def body(forward_prop, backward_prop, gamma_table, source_site, momenta):
    sizes = (forward_prop.shape, lax.axis_size("sx"), lax.axis_size("sy"))
    fits = sizes == ((2, 2, 12, 12, 8, 16 * LZ), 8, 4) and L == 64 and LZ == 64
    fits = fits and gamma_table.shape[0] == 16 and momenta.shape[0] == 32
    run = block_body if fits else general_body
    return run(forward_prop, backward_prop, gamma_table, source_site, momenta)


def solution(mesh):
    placed = (
        P(None, None, None, None, "sx", "sy"),
        P(None, None, None, None, "sx", "sy"),
        P(),
        P(),
        P(),
    )
    return jax.shard_map(
        body,
        mesh=mesh,
        in_specs=placed,
        out_specs=(P(None, None, None, "sx", "sy"), P()),
        check_vma=False,
    )
```

```python
import functools
import math

import jax
import jax.numpy as jnp
import numpy as np
from jax import lax
from jax.experimental import pallas as pl
from jax.experimental.pallas import tpu as pltpu
from jax.sharding import PartitionSpec as P

L = 64
LZ = 64


HIGHEST = lax.Precision.HIGHEST


def gamma_matrices(gamma_table):
    inserts = gamma_table.shape[0]
    columns = gamma_table[:, :, 0]
    powers = gamma_table[:, :, 1]
    spin_ids = jnp.arange(4, dtype=jnp.int32)
    matches = (columns[:, :, None] == spin_ids[None, None, :]).astype(jnp.float32)
    unit_re = (powers == 0).astype(jnp.float32) - (powers == 2).astype(jnp.float32)
    unit_im = (powers == 1).astype(jnp.float32) - (powers == 3).astype(jnp.float32)
    return (
        (matches * unit_re[:, :, None]).reshape(inserts, 16),
        (matches * unit_im[:, :, None]).reshape(inserts, 16),
    )


def dft_table(length, anchor):
    wavenum = jnp.arange(length, dtype=jnp.int32)
    offsets = jnp.mod(wavenum - anchor, length)
    phase_index = jnp.mod(offsets[:, None] * wavenum[None, :], length)
    angles = 2.0 * math.pi / length * phase_index.astype(jnp.float32)
    return (jnp.cos(angles), -jnp.sin(angles))


def complex_step(real_part, imag_part, table_re, table_im, pattern):
    out_re = jnp.einsum(pattern, real_part, table_re, precision=HIGHEST) - jnp.einsum(
        pattern, imag_part, table_im, precision=HIGHEST
    )
    out_im = jnp.einsum(pattern, real_part, table_im, precision=HIGHEST) + jnp.einsum(
        pattern, imag_part, table_re, precision=HIGHEST
    )
    return (out_re, out_im)


def transform(fields, source_site):
    table_re, table_im = dft_table(fields.shape[4], source_site[2])
    along_z = jnp.stack(
        complex_step(fields[:, 0], fields[:, 1], table_re, table_im, "nabz,zk->nabk"), 1
    )
    depth_share = along_z.shape[4] // lax.axis_size("sy")
    first_depth = lax.axis_index("sy") * depth_share
    length_y = along_z.shape[3] * lax.axis_size("sy")
    full_re, full_im = dft_table(length_y, source_site[1])
    part = lax.dynamic_slice_in_dim(
        lax.all_gather(along_z, "sy", axis=3, tiled=True), first_depth, depth_share, 4
    )
    step_re, step_im = complex_step(part[:, 0], part[:, 1], full_re, full_im, "nayc,yk->nakc")
    along_y = jnp.stack([step_re, step_im], 1)
    arrived = lax.all_to_all(along_y, "sx", split_axis=3, concat_axis=2, tiled=True)
    table_re, table_im = dft_table(arrived.shape[2], source_site[0])
    along_x = complex_step(arrived[:, 0], arrived[:, 1], table_re, table_im, "nxbc,xk->nbck")
    return jnp.stack(along_x, 1)


def apply_gammas(mat_re, mat_im, real_part, imag_part):
    extent = real_part.shape
    flat_re = real_part.reshape(extent[0], -1)
    flat_im = imag_part.reshape(extent[0], -1)
    out_re = jnp.dot(mat_re, flat_re, precision=HIGHEST) - jnp.dot(
        mat_im, flat_im, precision=HIGHEST
    )
    out_im = jnp.dot(mat_re, flat_im, precision=HIGHEST) + jnp.dot(
        mat_im, flat_re, precision=HIGHEST
    )
    return (out_re.reshape(extent), out_im.reshape(extent))


def project_sites(fields, source_site, momenta, rows_x, rows_y, length, depth):
    coord_x = lax.axis_index("sx") * rows_x + jnp.arange(rows_x, dtype=jnp.int32) - source_site[0]
    coord_y = lax.axis_index("sy") * rows_y + jnp.arange(rows_y, dtype=jnp.int32) - source_site[1]
    coord_z = jnp.arange(depth, dtype=jnp.int32) - source_site[2]
    part_x = jnp.mod(momenta[:, 0:1] * coord_x[None, :], length)
    part_y = jnp.mod(momenta[:, 1:2] * coord_y[None, :], length)
    part_z = jnp.mod(momenta[:, 2:3] * coord_z[None, :], depth)
    plane = jnp.mod(part_x[:, :, None] + part_y[:, None, :], length).astype(jnp.float32)
    angles = (
        2.0 * math.pi / length * plane[:, :, :, None]
        + 2.0 * math.pi / depth * part_z.astype(jnp.float32)[:, None, None, :]
    )
    angles = angles.reshape(momenta.shape[0], -1)
    cosine = jnp.cos(angles)
    sine = jnp.sin(angles)
    field_re = fields[:, 0].reshape(fields.shape[0], -1)
    field_im = fields[:, 1].reshape(fields.shape[0], -1)
    local_re = jnp.dot(field_re, cosine.T, precision=HIGHEST) + jnp.dot(
        field_im, sine.T, precision=HIGHEST
    )
    local_im = jnp.dot(field_im, cosine.T, precision=HIGHEST) - jnp.dot(
        field_re, sine.T, precision=HIGHEST
    )
    return (local_re, local_im)


def general_body(forward_prop, backward_prop, gamma_table, source_site, momenta):
    slices = forward_prop.shape[0]
    rows_x = forward_prop.shape[4]
    rows_y = backward_prop.shape[5] // LZ
    inserts = gamma_table.shape[0]
    forward = forward_prop.reshape(slices, 2, 4, 3, 12, -1)
    backward = backward_prop.reshape(slices, 2, 4, 3, 12, -1)
    pattern = "tscjn,tucjn->sutn"
    pair_re = jnp.einsum(
        pattern, backward[:, 0], forward[:, 0], preferred_element_type=jnp.float32
    ) + jnp.einsum(pattern, backward[:, 1], forward[:, 1], preferred_element_type=jnp.float32)
    pair_im = jnp.einsum(
        pattern, backward[:, 0], forward[:, 1], preferred_element_type=jnp.float32
    ) - jnp.einsum(pattern, backward[:, 1], forward[:, 0], preferred_element_type=jnp.float32)
    pair_re = pair_re.reshape(16, slices, -1)
    pair_im = pair_im.reshape(16, slices, -1)
    mat_re, mat_im = gamma_matrices(gamma_table)
    field_re, field_im = apply_gammas(mat_re, mat_im, pair_re, pair_im)
    fields = jnp.stack([field_re, field_im], 2).reshape(inserts * slices, 2, rows_x, rows_y, LZ)
    spectrum = transform(fields, source_site)
    local_re, local_im = project_sites(fields, source_site, momenta, rows_x, rows_y, L, LZ)
    listed_re, listed_im = lax.psum((local_re, local_im), ("sx", "sy"))
    listed_re = listed_re.reshape(inserts, slices, -1)
    listed_im = listed_im.reshape(inserts, slices, -1)
    corr_re = spectrum[:, 0].reshape(inserts, slices, spectrum.shape[2], -1)
    corr_im = spectrum[:, 1].reshape(inserts, slices, spectrum.shape[2], -1)
    return (jnp.stack([corr_re, corr_im], 2), jnp.stack([listed_re, listed_im], 0))


F32 = jnp.float32
BF16 = jnp.bfloat16
MIB = 2**20
SX_ORDER = (0, 4, 2, 6, 1, 5, 3, 7)


def split(values):
    high = values.astype(BF16)
    return (high, (values - high.astype(F32)).astype(BF16))


def turn(out_wave, in_site):
    angle = 2.0 * math.pi / L * np.mod(np.multiply.outer(out_wave, in_site), L)
    cosine, sine = (np.cos(angle), np.sin(angle))
    table = np.empty((len(out_wave), 2, 2, len(in_site)))
    table[:, 0, 0] = cosine
    table[:, 0, 1] = sine
    table[:, 1, 0] = -sine
    table[:, 1, 1] = cosine
    return table


def table_z():
    wave = turn(np.arange(64), np.arange(64)).reshape(4, 2, 4, 2, 2, 2, 64)
    full = np.zeros((4, 2, 4, 2, 2, 2, 2, 2, 64))
    for y in range(2):
        full[:, :, :, :, :, y, :, y, :] = wave
    return jnp.asarray(full.reshape(4, 64, 256).astype(np.float32))


def table_y():
    wave = turn(np.arange(64), np.arange(64)).reshape(8, 8, 2, 2, 4, 8, 2)
    full = np.zeros((4, 8, 2, 2, 8, 4, 8, 2, 2, 2))
    for position in range(4):
        for step in range(4):
            source = position ^ step
            for p in range(2):
                full[position, :, p, :, :, step, :, p] = wave[:, :, :, :, source].transpose(
                    0, 2, 1, 4, 3, 5
                )
    return jnp.asarray(full.reshape(4, 256, 256).astype(np.float32))


def table_x():
    wave = turn(np.arange(64), np.arange(64))
    cosine, sine = (wave[:, 0, 0].T, wave[:, 0, 1].T)
    table = np.concatenate([cosine, cosine, sine, sine], 1).astype(np.float32)
    return jnp.asarray(table.reshape(8, 8, 256))


def nt_dot(a, b):
    return lax.dot_general(a, b, (((1,), (1,)), ((), ())), preferred_element_type=F32)


def nn_dot(a, b):
    return lax.dot_general(a, b, (((1,), (0,)), ((), ())), preferred_element_type=F32)


def tn_dot(a, b):
    return lax.dot_general(a, b, (((0,), (0,)), ((), ())), preferred_element_type=F32)


def whole(shape):
    return pl.BlockSpec(shape, lambda step: (0,) * len(shape))


def cost(weight):
    return pl.CostEstimate(flops=weight * 10**13, bytes_accessed=0, transcendentals=0)


def contract_block(f_ref, b_ref, lanes):
    def add(total, term):
        return term if total is None else total + term

    def load(ref, ri, row, pair):
        both = ref[0, ri, row, 2 * pair : 2 * pair + 2, :, lanes].astype(F32)
        return (both[0], both[1])

    one, two, three = ([None] * 16, [None] * 16, [None] * 16)
    for colour in range(3):
        for pair in range(6):
            back = [[load(b_ref, ri, 3 * s + colour, pair) for ri in (0, 1)] for s in range(4)]
            forw = [[load(f_ref, ri, 3 * u + colour, pair) for ri in (0, 1)] for u in range(4)]
            for h in (0, 1):
                for s in range(4):
                    b_re, b_im = (back[s][0][h], back[s][1][h])
                    b_less, b_more = (b_re - b_im, b_re + b_im)
                    for u in range(4):
                        f_re, f_im = (forw[u][0][h], forw[u][1][h])
                        f_more = f_re + f_im
                        k = 4 * s + u
                        one[k] = add(one[k], b_re * f_more)
                        two[k] = add(two[k], b_less * f_im)
                        three[k] = add(three[k], b_more * f_re)
    return [(one[k] - two[k], one[k] - three[k]) for k in range(16)]


def phases(index):
    half = (((index + 32) & 63) - 32).astype(F32) * (math.pi / 64)
    square = half * half
    sine = jnp.full_like(square, -1 / math.factorial(11))
    for n in (9, 7, 5, 3, 1):
        sine = sine * square + (-1) ** (n // 2) / math.factorial(n)
    sine = sine * half
    cosine = jnp.full_like(square, 1 / math.factorial(12))
    for n in (10, 8, 6, 4, 2, 0):
        cosine = cosine * square + (-1) ** (n // 2) / math.factorial(n)
    return (1.0 - 2.0 * sine * sine, 2.0 * sine * cosine)


def iota(shape, dim):
    return lax.broadcasted_iota(jnp.int32, shape, dim)


def planes(ref, lanes):
    re_high, re_low = split(ref[:, 0, :, lanes].reshape(128, 128))
    im_high, im_low = split(ref[:, 1, :, lanes].reshape(128, 128))
    return (jnp.concatenate([re_high, im_high], 1), jnp.concatenate([re_low, im_low], 1))


def momentum_lanes(mom_ref):
    lane = iota((1, 128), 1) & 31
    rows = []
    for k in range(3):
        row = jnp.zeros((1, 128), jnp.int32)
        for m in range(32):
            row = jnp.where(lane == m, mom_ref[k, m], row)
        rows.append(row)
    return rows


def momentum_tables(mom_ref, tm_high_ref, tm_low_ref):
    _, mom_y, mom_z = momentum_lanes(mom_ref)
    out_part = ((iota((64, 128), 1) >> 5) & 1) == 1
    for y in range(2):
        cosine, sine = phases(mom_z * iota((64, 128), 0) + mom_y * y)
        less = jnp.where(out_part, cosine, sine)
        none = jnp.where(out_part, -sine, cosine)
        more = jnp.where(out_part, -cosine, -sine)
        for part_in, blocks in ((0, (none, more)), (1, (less, none))):
            for turned in range(2):
                high, low = split(blocks[turned])
                rows = pl.ds(128 * part_in + 64 * y, 64)
                lanes = pl.ds(128 * turned, 128)
                tm_high_ref[rows, lanes] = high
                tm_low_ref[rows, lanes] = low


def pair_kernel(listed, aliased, source_ref, mom_ref, f_ref, b_ref, wave_ref, *refs):
    if aliased:
        refs = refs[1:]
    if listed:
        old_ref, *sends, field_ref, w_high_ref, w_low_ref = refs[:8]
        tm_high_ref, tm_low_ref, total_ref = refs[8:]
    else:
        *sends, fields_ref, field_ref, w_high_ref, w_low_ref = refs
    step = pl.program_id(0)
    steps = pl.num_programs(0) - 1
    parts = f_ref.shape[5] // 128

    @pl.when(step == 0)
    def _():
        blocks = [lax.axis_index("sy") ^ s for s in range(4)]
        high, low = split(jnp.concatenate([wave_ref[block] for block in blocks], 0))
        w_high_ref[...] = high
        w_low_ref[...] = low
        if listed:
            momentum_tables(mom_ref, tm_high_ref, tm_low_ref)
            total_ref[...] = jnp.zeros_like(total_ref)

    def project(t, high, low, row, there):
        proj = (
            nn_dot(high, tm_high_ref[...])
            + nn_dot(high, tm_low_ref[...])
            + nn_dot(low, tm_high_ref[...])
        )
        value, turned = (proj[:, :128], proj[:, 128:])
        cosine, sine = phases(2 * momentum_lanes(mom_ref)[1] * row)
        total_ref[t, 0] += jnp.where(there, cosine * value + sine * turned, 0.0)
        total_ref[t, 1] += jnp.where(there, cosine * turned - sine * value, 0.0)

    def transform(row, there):
        high, low = planes(field_ref, pl.ds(0, 128))
        w_high, w_low = (w_high_ref[...], w_low_ref[...])
        out = nt_dot(w_high, high) + nt_dot(w_low, high) + nt_dot(w_high, low)
        halves = len(sends) // 4
        count = 8 // halves
        out = out.reshape(4, halves, count, 8, 128)
        for s in range(4):
            for h in range(halves):
                sends[4 * h + s][pl.ds(count * row, count)] = out[s, h]
        if listed:
            project(1, high, low, row, there)

    @pl.when(step < steps)
    def _():
        for part in range(parts):
            lanes = pl.ds(128 * part, 128)
            row = parts * step + part
            transform(jnp.maximum(row - 1, 0), row > 0)
            if listed:
                project(0, *planes(old_ref, lanes), row, True)
            for k, (real, imag) in enumerate(contract_block(f_ref, b_ref, lanes)):
                field_ref[k, 0] = real
                field_ref[k, 1] = imag
                if not listed:
                    fields_ref[k, 0, :, lanes] = real
                    fields_ref[k, 1, :, lanes] = imag

    @pl.when(step == steps)
    def _():
        transform(parts * steps - 1, True)
        if listed:
            mom_x, mom_y, mom_z = momentum_lanes(mom_ref)
            x = lax.axis_index("sx") * 8 - source_ref[0] + iota((8, 128), 0)
            rest = (lax.axis_index("sy") * 16 - source_ref[1]) * mom_y - source_ref[2] * mom_z
            cosine, sine = phases(x * mom_x + rest)
            for t in range(2):
                value = total_ref[t, 0].reshape(16, 8, 128)
                turned = total_ref[t, 1].reshape(16, 8, 128)
                summed = jnp.sum(value * cosine[None] + turned * sine[None], 1)
                tile = jnp.where(iota((8, 128), 1) >= 64, summed[8:], summed[:8])
                for s in range(4):
                    sends[s][64 + t] = tile


def pair_call(which, start, rows, parts, listed, fields, forward, backward, wave, source_site, momenta):
    steps = rows // parts
    lanes = 128 * parts

    def block(step):
        return (which, 0, 0, 0, 0, start // parts + jnp.minimum(step, steps - 1))

    in_specs = [pl.BlockSpec(memory_space=pltpu.SMEM)] * 2
    in_specs += [pl.BlockSpec((1, 2, 12, 12, 8, lanes), block)] * 2 + [whole((4, 64, 256))]
    operands = [source_site, momenta, forward, backward, wave]
    shapes = [(8 * rows + 2 if listed else 8 * rows, 8, 128)] * 4
    out_specs = [whole(shape) for shape in shapes]
    scratch = [pltpu.VMEM((16, 2, 8, 128), F32)] + [pltpu.VMEM((256, 256), BF16)] * 2
    aliases = {}
    if listed:
        in_specs.append(
            pl.BlockSpec((16, 2, 8, lanes), lambda step: (0, 0, 0, block(step)[5]))
        )
        operands.append(fields)
        scratch += [pltpu.VMEM((256, 256), BF16)] * 2 + [pltpu.VMEM((2, 2, 128, 128), F32)]
    else:
        shapes.append((16, 2, 8, 1024))
        out_specs.append(pl.BlockSpec((16, 2, 8, lanes), lambda step: (0, 0, 0, block(step)[5])))
        if fields is not None:
            in_specs.append(pl.BlockSpec(memory_space=pl.ANY))
            operands.append(fields)
            aliases = {5: 4}
    return pl.pallas_call(
        functools.partial(pair_kernel, listed, bool(aliases)),
        grid=(steps + 1,),
        in_specs=in_specs,
        out_specs=out_specs,
        out_shape=[jax.ShapeDtypeStruct(shape, F32) for shape in shapes],
        scratch_shapes=scratch,
        input_output_aliases=aliases,
        compiler_params=pltpu.CompilerParams(vmem_limit_bytes=55 * MIB),
        cost_estimate=cost(0),
        name="contract_and_z",
    )(*operands)


def y_kernel(parts, listed, apart, kept, *refs):
    messages = [refs[s + 4 * part] for s in range(4) for part in range(parts)]
    if kept:
        refs[-2][...] = refs[4 * parts + 1][...]
        refs = refs[: 4 * parts + 1] + refs[4 * parts + 2 : -2] + refs[-1:]
    wave_ref, *sends, work_ref = refs[4 * parts :]
    if not apart:
        sends = [sends[0].at[k] for k in range(8)]
    w_high, w_low = split(wave_ref[0])
    for q in range(0, 8, 2):
        data = [
            jnp.concatenate([ref[8 * y + q], ref[8 * y + q + 1]], 1)
            for ref in messages
            for y in range(ref.shape[0] // 8)
        ]
        high, low = split(jnp.concatenate(data, 0))
        out = nn_dot(w_high, high) + nn_dot(w_low, high) + nn_dot(w_high, low)
        work_ref[q] = out[:, :128].reshape(8, 2, 2, 8, 128)
        work_ref[q + 1] = out[:, 128:].reshape(8, 2, 2, 8, 128)
    for h in range(2):
        for step in range(8):
            block = lax.axis_index("sx") ^ step if apart else step
            tiles = [
                work_ref[4 * h + q, block, p, ri]
                for ri in range(2)
                for q in range(4)
                for p in range(2)
            ]
            turned = jnp.concatenate(tiles, 0).T.reshape(16, 8, 128)
            sends[step][pl.ds(16 * h, 16)] = turned
    if listed:
        for t in range(2):
            share = sum(ref[64 + t] for ref in messages)
            for step in range(8):
                sends[step][32 + t] = share


def y_call(listed, apart, weight, parts, wave, kept=None):
    messages = [x for part in parts for x in part]
    tiles = 34 if listed else 32
    shapes = [(tiles, 8, 128)] * 8 if apart else [(8, tiles, 8, 128)]
    extra = [] if kept is None else [kept]
    shapes += [x.shape for x in extra]
    return pl.pallas_call(
        functools.partial(y_kernel, len(parts), listed, apart, kept is not None),
        grid=(1,),
        in_specs=[whole(x.shape) for x in messages]
        + [pl.BlockSpec((1, 256, 256), lambda step: (lax.axis_index("sy"), 0, 0))]
        + [whole(x.shape) for x in extra],
        out_specs=[whole(shape) for shape in shapes],
        out_shape=[jax.ShapeDtypeStruct(shape, F32) for shape in shapes],
        scratch_shapes=[pltpu.VMEM((8, 8, 2, 2, 8, 128), F32)],
        compiler_params=pltpu.CompilerParams(vmem_limit_bytes=32 * MIB),
        cost_estimate=cost(weight),
        name="along_y",
    )(*messages, wave, *extra)


def x_kernel(count, listed, table_ref, source_ref, rows_ref, wave_ref, *refs):
    data_refs, work_ref = (refs[:count], refs[-1])
    out_ref = refs[-3] if listed else refs[-2]
    listed_ref = refs[-2] if listed else None
    if count == 1:
        data_refs = [data_refs[0].at[k] for k in range(8)]
    half = pl.program_id(0)
    first_x, first_y = (lax.axis_index("sx") * 8, lax.axis_index("sy") * 16)
    blocks = range(8) if count == 1 else [lax.axis_index("sx") ^ k for k in SX_ORDER]
    w_high, w_low = split(jnp.concatenate([wave_ref[block] for block in blocks], 0))
    weights = jnp.concatenate([w_high, w_high, w_low], 0)
    lower = iota((8, 128), 1) < 64
    for f in range(16):
        if f % 4 == 0:
            data = []
            for k in range(f, f + 4):
                parts = [ref[16 * half + k] for ref in data_refs]
                high, low = split(jnp.concatenate(parts, 0))
                data.append(jnp.concatenate([high, low, high], 0))
            group = tn_dot(jnp.concatenate(data, 1), weights)
        out = group[128 * (f % 4) : 128 * (f % 4 + 1)]
        cosine = out[:, :128].reshape(2, 4, 2, 8, 128)
        sine = out[:, 128:].reshape(2, 4, 2, 8, 128)
        real = cosine[0] + sine[1]
        imag = cosine[1] - sine[0]
        for q in range(4):
            lanes = pl.ds(128 * q, 128)
            work_ref[f, 0, :, lanes] = jnp.where(lower, real[q, 0], real[q, 1])
            work_ref[f, 1, :, lanes] = jnp.where(lower, imag[q, 0], imag[q, 1])
    column = iota((8, 512), 1)
    index = (first_x + iota((8, 512), 0)) * source_ref[1] + (column & 63) * source_ref[0]
    cosine, sine = phases(index + (first_y + 8 * half + (column >> 6)) * source_ref[2])
    for g in range(16):
        real = jnp.zeros((8, 512), F32)
        imag = jnp.zeros((8, 512), F32)
        for s in range(4):
            field = 4 * s + table_ref[8 * g + 2 * s]
            power = table_ref[8 * g + 2 * s + 1]
            odd = power & 1
            sign_re = jnp.where((power == 0) | (power == 3), 1.0, -1.0).astype(F32)
            sign_im = jnp.where(power < 2, 1.0, -1.0).astype(F32)
            real += sign_re * work_ref[field, odd]
            imag += sign_im * work_ref[field, 1 - odd]
        out_ref[g, 0, 0] = real * cosine - imag * sine
        out_ref[g, 0, 1] = real * sine + imag * cosine

    def listed_sums():
        mix = mix_matrix(rows_ref[...]).astype(BF16)
        for t in range(2):
            total = sum(ref[32 + t] for ref in data_refs)
            rows = jnp.concatenate([total[:, 32 * k : 32 * k + 32] for k in range(4)], 0)
            high, rest = split(rows)
            middle, low = split(rows - high.astype(F32))
            sums = nn_dot(mix, high) + nn_dot(mix, middle) + nn_dot(mix, low)
            for ri in range(2):
                for g in range(16):
                    row = 16 * ri + g
                    listed_ref[ri, g, t : t + 1] = sums[row : row + 1]

    if listed:
        pl.when(half == 0)(listed_sums)


def x_call(which, data, gammas, rows, source_site, wave, corr):
    if len(data) == 8:
        data = [data[k] for k in SX_ORDER]
    in_specs = [
        pl.BlockSpec(memory_space=pltpu.SMEM),
        pl.BlockSpec(memory_space=pltpu.SMEM),
        whole((16, 8)),
        whole((8, 8, 256)),
    ] + [whole(x.shape) for x in data]
    operands = [gammas, source_site, rows, wave, *data]
    aliases = {}
    shapes = [(16, 2, 2, 8, 1024)]
    out_specs = [pl.BlockSpec((16, 1, 2, 8, 512), lambda step: (0, which, 0, 0, step))]
    if corr is not None:
        aliases = {len(operands): 0}
        in_specs.append(pl.BlockSpec(memory_space=pl.ANY))
        operands.append(corr)
        shapes.append((2, 16, 2, 32))
        out_specs.append(whole(shapes[1]))
    return pl.pallas_call(
        functools.partial(x_kernel, len(data), corr is not None),
        grid=(2,),
        in_specs=in_specs,
        out_specs=out_specs,
        out_shape=[jax.ShapeDtypeStruct(shape, F32) for shape in shapes],
        scratch_shapes=[pltpu.VMEM((16, 2, 8, 512), F32)],
        input_output_aliases=aliases,
        compiler_params=pltpu.CompilerParams(vmem_limit_bytes=32 * MIB),
        cost_estimate=cost(0),
        name="along_x",
    )(*operands)


def mix_matrix(gammas):
    column = iota((16, 32), 1)
    field = (column >> 4) * 8 + (column & 7)
    on_imag = ((column >> 3) & 1) == 1
    real = jnp.zeros((16, 32), F32)
    imag = jnp.zeros((16, 32), F32)
    for s in range(4):
        match = field == 4 * s + gammas[:, 2 * s : 2 * s + 1]
        power = gammas[:, 2 * s + 1 : 2 * s + 2]
        unit_re = (power == 0).astype(F32) - (power == 2).astype(F32)
        unit_im = (power == 1).astype(F32) - (power == 3).astype(F32)
        real += jnp.where(match, jnp.where(on_imag, -unit_im, unit_re), 0.0)
        imag += jnp.where(match, jnp.where(on_imag, unit_re, unit_im), 0.0)
    return jnp.concatenate([real, imag], 0)


def swap_sy(message):
    out = list(message)
    for step in (3, 2, 1):
        out[step] = lax.ppermute(message[step], "sy", [(k, k ^ step) for k in range(4)])
    return out


def swap_sx_whole(message):
    return [lax.all_to_all(message[0], "sx", 0, 0, tiled=True)]


def swap_sx(message):
    out = list(message)
    for step in SX_ORDER[1:]:
        out[step] = lax.ppermute(message[step], "sx", [(k, k ^ step) for k in range(8)])
    return out


def after(values, *others):
    return lax.optimization_barrier((values, others))[0]


def block_body(forward_prop, backward_prop, gamma_table, source_site, momenta):
    wave_z, wave_y, wave_x = (table_z(), table_y(), table_x())
    site, mom = (source_site, momenta.T)
    outer = (gamma_table.reshape(-1), gamma_table.reshape(16, 8), source_site, wave_x)
    *first, fields = pair_call(0, 0, 3, 1, False, None, forward_prop, backward_prop, wave_z, site, mom)
    site, first = after((site, first))
    first = swap_sy(first)
    *third, fields = pair_call(0, 3, 5, 1, False, fields, forward_prop, backward_prop, wave_z, site, mom)
    site, third = after((site, third))
    first, third[1] = after((first, third[1]))
    third = swap_sy(third)
    second = list(pair_call(1, 0, 8, 2, True, fields, forward_prop, backward_prop, wave_z, site, mom))
    third, second[1] = after((third, second[1]))
    second = swap_sy(second)
    *sent, second[0] = y_call(False, False, 0, [first, third], wave_y, second[0])
    data = swap_sx_whole(sent)
    second[1:] = after(second[1:], sent[0])
    sent = y_call(True, True, 1, [second], wave_y)
    data = after(data, sent[0])
    (corr,) = x_call(0, data, *outer, None)
    second = swap_sx(sent)
    corr, listed = x_call(1, second, *outer, corr)
    return (corr, listed)


def body(forward_prop, backward_prop, gamma_table, source_site, momenta):
    sizes = (forward_prop.shape, lax.axis_size("sx"), lax.axis_size("sy"))
    fits = sizes == ((2, 2, 12, 12, 8, 16 * LZ), 8, 4) and L == 64 and LZ == 64
    fits = fits and gamma_table.shape[0] == 16 and momenta.shape[0] == 32
    run = block_body if fits else general_body
    return run(forward_prop, backward_prop, gamma_table, source_site, momenta)


def solution(mesh):
    placed = (
        P(None, None, None, None, "sx", "sy"),
        P(None, None, None, None, "sx", "sy"),
        P(),
        P(),
        P(),
    )
    return jax.shard_map(
        body,
        mesh=mesh,
        in_specs=placed,
        out_specs=(P(None, None, None, "sx", "sy"), P()),
        check_vma=False,
    )
```
